512 devices in a mesh: tm: 128 (over y, z, core), space: 4 (over x).
Axes of the slice: x: 4, y: 8, z: 8, core: 2. Of those that a mesh axis runs over, the one named last changes fastest.
Arguments:
- video: bfloat16 [128, 8, 8, 16, 128], P('tm', None, 'space'), may hold values from -6 to 6
- cotangent: bfloat16 [128, 8, 8, 16, 128], P('tm', None, 'space'), may hold values from -6 to 6
- weight_one: bfloat16 [3456, 128], replicated, may hold values from -0.109375 to 0.109375
- weight_two: bfloat16 [3456, 128], replicated, may hold values from -0.109375 to 0.109375
- predecessor: int32 [128], P('tm'), may hold values from -1 to 126, as said below
- frame_count: int32 [128], P('tm'), may hold values from 1 to 8, as said below
Outputs:
- output: bfloat16 [128, 8, 8, 16, 128], P('tm', None, 'space')
- grad_one: float32 [3456, 128], P('space')
- grad_two: float32 [3456, 128], P('space')
The draws below stay inside these ranges and needn't reach their ends.
Inputs may be any that keep to these rules, and one draw needn't show every extreme that they name: predecessor[c] is c - 1, or -1 where group c starts a clip; group 0 starts a clip and group 1 continues it. `frame_count`: a group with fewer than 8 frames is the last group or is followed by a group that starts a clip; the last group has fewer than 8 frames.
All inputs are finite; a program needn't handle non-finite values.
Results may differ from the reference program's by a relative error of at most 0.006.
Values may be sent and summed in bfloat16 or wider, within the bound.
A program may use at most 64 MiB of HBM per device.

```python
import math
import jax
import jax.numpy as jnp
from jax import lax

C = 128
FR = 8
TAPS = 27
WW = 16
GROUPS = 128
NH = 8
VOXELS = 131072


def clip_starts(key):
    flags = jax.random.randint(key, (GROUPS,), 0, 4) == 0
    index = jnp.arange(GROUPS, dtype=jnp.int32)
    inner = jnp.where((index == 1) | (index == GROUPS - 1), False, flags)
    return jnp.where(index == 0, True, inner)


def draw_predecessor(key, part):
    starts = clip_starts(key)
    index = jnp.arange(GROUPS, dtype=jnp.int32)
    return jnp.where(starts, -1, index - 1).astype(jnp.int32)


def draw_frame_count(key, part):
    starts = clip_starts(key)
    key = jax.random.fold_in(key, 12)
    index = jnp.arange(GROUPS, dtype=jnp.int32)
    following = jnp.concatenate([starts[1:], jnp.ones((1,), dtype=bool)])
    shorter = jax.random.randint(key, (GROUPS,), 1, FR + 1)
    last_count = jax.random.randint(jax.random.fold_in(key, 5), (GROUPS,), 1, FR)
    counts = jnp.where(following, shorter, FR)
    return jnp.where(index == GROUPS - 1, last_count, counts).astype(jnp.int32)


def block_scale(own_key, shape, split, least, largest):
    level, own = 1.0, jax.random.fold_in(own_key, 6)
    for position, blocks in split:
        heights = jnp.exp(jax.random.uniform(jax.random.fold_in(own, position), (blocks,), jnp.float32, least / len(split), largest / len(split)))
        level = level * jnp.repeat(heights, shape[position] // blocks).reshape([-1 if axis == position else 1 for axis in range(len(shape))])
    return level


def bell_draw(stream_key, shape, deviation, bound, shards=(), kind=jnp.bfloat16):
    level = block_scale(stream_key, shape, shards, -0.22, 0.18) if shards else 1.0
    values = jax.random.normal(stream_key, shape, jnp.float32) * deviation * level
    return jnp.minimum(jnp.maximum(values, -bound), bound).astype(kind)


def setup_inputs(seed: int = 0) -> dict:
    key_of = jax.random.split(jax.random.key(seed), 7)
    video = bell_draw(key_of[0], (GROUPS, FR, NH, WW, C), 1.0, 6.0, ((0, 128), (2, 4)))
    cotangent = bell_draw(key_of[1], (GROUPS, FR, NH, WW, C), 1.0, 6.0, ((0, 128), (2, 4)))
    weight_one = bell_draw(key_of[2], (TAPS * C, C), (TAPS * C) ** -0.5, 0.109375)
    weight_two = bell_draw(key_of[3], (TAPS * C, C), (TAPS * C) ** -0.5, 0.109375)
    predecessor = draw_predecessor(jax.random.fold_in(key_of[6], 71), 0)
    frame_count = draw_frame_count(jax.random.fold_in(key_of[6], 71), 0)
    return {"video": video, "cotangent": cotangent, "weight_one": weight_one, "weight_two": weight_two, "predecessor": predecessor, "frame_count": frame_count}


def build_patches(extended, frames, height, columns):
    pieces = []
    for depth in range(3):
        for down in range(3):
            for across in range(3):
                pieces.append(extended[depth:depth + frames, down:down + height, across:across + columns, :])
    stacked = jnp.concatenate(pieces, axis=-1)
    return stacked.reshape(frames * height * columns, stacked.shape[-1])

def silu_slope(value):
    sigma = jax.nn.sigmoid(value)
    return sigma * (1.0 + value * (1.0 - sigma))

def contract(patches, delta):
    return lax.dot_general(patches, delta, (((0,), (0,)), ((), ())), preferred_element_type=jnp.float32)

def extend(field, starting):
    earlier = jnp.roll(field, 1, axis=0)[:, FR - 2:]
    own_first = jnp.concatenate([field[:, :1], field[:, :1]], axis=1)
    cache = jnp.where(starting[:, None, None, None, None], own_first, earlier)
    joined = jnp.concatenate([cache, field], axis=1)
    return jnp.pad(joined, ((0, 0), (0, 0), (1, 1), (1, 1), (0, 0)))

def convolve(extended, weight):

    def one_group(piece):
        result = jnp.dot(build_patches(piece, FR, NH, WW), weight, preferred_element_type=jnp.float32)
        return result.reshape(FR, NH, WW, C)
    return lax.map(one_group, extended)

def reference(video, cotangent, weight_one, weight_two, predecessor, frame_count):
    starting = predecessor < 0
    live = (jnp.arange(FR)[None, :] < frame_count[:, None]).astype(jnp.float32)[:, :, None, None, None]
    scale = 1.0 / math.sqrt(VOXELS)
    ext_one = extend(video, starting)
    first_act = convolve(ext_one, weight_one)
    hidden = (live * jax.nn.silu(first_act)).astype(jnp.bfloat16)
    ext_two = extend(hidden, starting)
    second_act = convolve(ext_two, weight_two)
    output = (live * (video.astype(jnp.float32) + second_act)).astype(jnp.bfloat16)
    delta_two = (live * cotangent.astype(jnp.float32)).astype(jnp.bfloat16)

    def backward_group(items):
        extended, delta = items
        flat = delta.reshape(-1, C)
        term = contract(build_patches(extended, FR, NH, WW), flat)
        back = lax.dot_general(flat, weight_two, (((1,), (1,)), ((), ())), preferred_element_type=jnp.float32)
        _, pull = jax.vjp(lambda grid: build_patches(grid, FR, NH, WW), jnp.zeros(extended.shape, jnp.float32))
        spread = pull(back)[0][:, 1:NH + 1, 1:WW + 1]
        return (term, spread)
    terms, spread = lax.map(backward_group, (ext_two, delta_two))
    grad_two = scale * lax.optimization_barrier(jnp.sum(terms, axis=0))
    cache_part = spread[:, :2]
    own = spread[:, 2:]
    passing = jnp.where(starting[:, None, None, None, None], 0.0, cache_part)
    own = own.at[:, FR - 2:].add(jnp.roll(passing, -1, axis=0))
    own = own.at[:, 0].add(jnp.where(starting[:, None, None, None], cache_part[:, 0] + cache_part[:, 1], 0.0))
    delta_one = (own * live * silu_slope(first_act)).astype(jnp.bfloat16)

    def weight_term(items):
        return contract(build_patches(items[0], FR, NH, WW), items[1].reshape(-1, C))
    grad_one = scale * lax.optimization_barrier(jnp.sum(lax.map(weight_term, (ext_one, delta_one)), axis=0))
    return (output, grad_one, grad_two)
```

```python
import math

import jax
import jax.numpy as jnp
from jax import lax
from jax.experimental import pallas as pl
from jax.experimental.pallas import tpu as pltpu
from jax.sharding import PartitionSpec as P

MESH = pl.DeviceIdType.MESH
SIDE = 8
BLOCK = 112
TILE = 16


def build_patches(extended, frames, height, columns):
    pieces = []
    for depth in range(3):
        for down in range(3):
            for across in range(3):
                pieces.append(
                    extended[
                        depth : depth + frames, down : down + height, across : across + columns, :
                    ]
                )
    stacked = jnp.concatenate(pieces, axis=-1)
    return stacked.reshape(frames * height * columns, stacked.shape[-1])


def silu_slope(value):
    sigma = jax.nn.sigmoid(value)
    return sigma * (1.0 + value * (1.0 - sigma))


def contract(patches, delta):
    return lax.dot_general(
        patches, delta, (((0,), (0,)), ((), ())), preferred_element_type=jnp.float32
    )


def passed_along(value, axis, steps):
    count = lax.axis_size(axis)
    initial, last = (max(0, -steps), min(count, count - steps))
    return lax.ppermute(value, axis, [(source, source + steps) for source in range(initial, last)])


def reduce_kernel(
    scale, part_ref, one_ref, two_ref,
    swap_out, swap_in, total, stage, land_a, stage_b, land_b, mine, tiles, wide, other,
    swap_send, swap_recv, a_send, a_recv, b_send, b_recv, tb_send, tb_recv,
    ta_send, ta_recv, o_send, o_recv,
):
    tm = lax.axis_index("tm")
    space = lax.axis_index("space")
    core = lax.rem(tm, 2)
    chip = tm // 2
    y, z = chip // SIDE, lax.rem(chip, SIDE)
    a = y * (1 - core) + z * core
    b = z * (1 - core) + y * core
    stride_a, stride_b = 8 - 7 * core, 1 + 7 * core
    rows = one_ref.shape[0]

    def along_a(step):
        at = lax.rem(a + step, SIDE)
        return at, (2 * (at * stride_a + b * stride_b) + core, space)

    def along_b(step):
        at = lax.rem(b + step, SIDE)
        return at, (2 * (a * stride_a + at * stride_b) + core, space)

    sibling = (tm + 1 - 2 * core, space)

    barrier = pltpu.get_barrier_semaphore()
    pl.semaphore_signal(barrier, inc=1, device_id=sibling, device_id_type=MESH)
    for step in range(1, SIDE):
        pl.semaphore_signal(barrier, inc=1, device_id=along_a(step)[1], device_id_type=MESH)
        pl.semaphore_signal(barrier, inc=1, device_id=along_b(step)[1], device_id_type=MESH)
    pl.semaphore_wait(barrier, 2 * SIDE - 1)

    def send(source, target, send_sem, recv_sem, device):
        copy = pltpu.make_async_remote_copy(
            src_ref=source, dst_ref=target, send_sem=send_sem, recv_sem=recv_sem,
            device_id=device, device_id_type=MESH,
        )
        copy.start()
        return copy

    swap_out[...] = part_ref[1 - core].astype(jnp.bfloat16)
    swap = send(swap_out, swap_in, swap_send, swap_recv, sibling)
    swap.wait_recv()
    total[0:rows] = part_ref[core] + swap_in[...].astype(jnp.float32)
    total[rows:] = jnp.zeros((SIDE * BLOCK - rows, total.shape[1]), jnp.float32)
    stage[...] = total[...].astype(jnp.bfloat16).reshape(stage.shape)

    over_a = []
    for step in range(1, SIDE):
        at, device = along_a(step)
        over_a.append(
            send(stage.at[at], land_a.at[step - 1], a_send.at[step - 1], a_recv.at[step - 1], device)
        )
    block = total[pl.ds(a * BLOCK, BLOCK)]
    for step in range(1, SIDE):
        over_a[step - 1].wait_recv()
        block = block + land_a[step - 1].astype(jnp.float32)
    total[0:BLOCK] = block
    total[BLOCK : BLOCK + TILE] = jnp.zeros((TILE, total.shape[1]), jnp.float32)
    stage_b[...] = total[0 : BLOCK + TILE].astype(jnp.bfloat16).reshape(stage_b.shape)

    over_b = []
    for step in range(1, SIDE):
        at, device = along_b(step)
        over_b.append(
            send(stage_b.at[at], land_b.at[step - 1], b_send.at[step - 1], b_recv.at[step - 1], device)
        )
    tile = total[pl.ds(b * TILE, TILE)]
    for step in range(1, SIDE):
        over_b[step - 1].wait_recv()
        tile = tile + land_b[step - 1].astype(jnp.float32)
    mine[...] = (tile * scale).astype(jnp.bfloat16)
    tiles[b] = mine[...]

    back_b = []
    for step in range(1, SIDE):
        at, device = along_b(step)
        back_b.append(
            send(mine, tiles.at[b], tb_send.at[step - 1], tb_recv.at[step - 1], device)
        )
    for step in range(1, SIDE):
        back_b[step - 1].wait_recv()
    wide[a] = tiles[0 : SIDE - 1].reshape(BLOCK, tiles.shape[-1])

    back_a = []
    for step in range(1, SIDE):
        at, device = along_a(step)
        back_a.append(
            send(wide.at[a], wide.at[a], ta_send.at[step - 1], ta_recv.at[step - 1], device)
        )
    across = [send(wide.at[a], other.at[a], o_send.at[0], o_recv.at[0], sibling)]
    for step in range(1, SIDE):
        back_a[step - 1].wait_recv()
        origin = lax.rem(a + SIDE - step, SIDE)
        across.append(
            send(wide.at[origin], other.at[origin], o_send.at[step], o_recv.at[step], sibling)
        )
    for copy in across:
        copy.wait_recv()
    full = wide[...].astype(jnp.float32).reshape(SIDE * BLOCK, -1)[0:rows]
    rest = other[...].astype(jnp.float32).reshape(SIDE * BLOCK, -1)[0:rows]
    one_ref[...] = jnp.where(core == 0, full, rest)
    two_ref[...] = jnp.where(core == 0, rest, full)
    for copy in [swap] + over_a + over_b + back_b + back_a + across:
        copy.wait_send()


def reduced(part, scale):
    rows, width = part.shape[1:]
    half = jnp.bfloat16
    full = jnp.float32
    dma = pltpu.SemaphoreType.DMA
    return pl.pallas_call(
        lambda *refs: reduce_kernel(scale, *refs),
        out_shape=(jax.ShapeDtypeStruct((rows, width), full),) * 2,
        in_specs=[pl.BlockSpec(memory_space=pltpu.VMEM)],
        out_specs=(pl.BlockSpec(memory_space=pltpu.VMEM),) * 2,
        scratch_shapes=[
            pltpu.VMEM((rows, width), half),
            pltpu.VMEM((rows, width), half),
            pltpu.VMEM((SIDE * BLOCK, width), full),
            pltpu.VMEM((SIDE, BLOCK, width), half),
            pltpu.VMEM((SIDE - 1, BLOCK, width), half),
            pltpu.VMEM((SIDE, TILE, width), half),
            pltpu.VMEM((SIDE - 1, TILE, width), half),
            pltpu.VMEM((TILE, width), half),
            pltpu.VMEM((SIDE, TILE, width), half),
            pltpu.VMEM((SIDE, BLOCK, width), half),
            pltpu.VMEM((SIDE, BLOCK, width), half),
            dma,
            dma,
            dma((SIDE - 1,)),
            dma((SIDE - 1,)),
            dma((SIDE - 1,)),
            dma((SIDE - 1,)),
            dma((SIDE - 1,)),
            dma((SIDE - 1,)),
            dma((SIDE - 1,)),
            dma((SIDE - 1,)),
            dma((SIDE,)),
            dma((SIDE,)),
        ],
        compiler_params=pltpu.CompilerParams(
            collective_id=0, has_side_effects=True, vmem_limit_bytes=32 * 1024 * 1024
        ),
    )(part)


def extend(field, starting):
    earlier = passed_along(field[field.shape[0] - 2 :], "tm", 1)
    own_first = jnp.concatenate([field[:1], field[:1]], axis=0)
    cache = jnp.where(starting, own_first, earlier)
    joined = jnp.concatenate([cache, field], axis=0)
    return jnp.pad(joined, ((0, 0), (1, 1), (1, 1), (0, 0)))


def per_device(video, cotangent, weight_one, weight_two, predecessor, frame_count):
    space = lax.axis_index("space")
    low = video.shape[2]
    both = lax.all_gather(jnp.concatenate([video, cotangent]), "space", axis=2, tiled=True)
    field, change = both[0], both[1]
    frames, height, columns, width = field.shape
    starting = predecessor[0] < 0
    live = (jnp.arange(frames) < frame_count[0]).astype(jnp.float32)[:, None, None, None]
    scale = 1.0 / math.sqrt(lax.axis_size("tm") * frames * height * columns)
    patches_one = build_patches(extend(field, starting), frames, height, columns)
    first_act = jnp.dot(patches_one, weight_one, preferred_element_type=jnp.float32).reshape(
        frames, height, columns, width
    )
    hidden = (live * jax.nn.silu(first_act)).astype(jnp.bfloat16)
    ext_two = extend(hidden, starting)
    patches_two = build_patches(ext_two, frames, height, columns)
    near = lax.dynamic_slice_in_dim(ext_two, space * low, low + 2, 1)
    second_act = jnp.dot(
        build_patches(near, frames, low, columns), weight_two, preferred_element_type=jnp.float32
    ).reshape(frames, low, columns, width)
    output = (live * (video[0].astype(jnp.float32) + second_act)).astype(jnp.bfloat16)
    delta_two = (live * change.astype(jnp.float32)).astype(jnp.bfloat16).reshape(-1, width)
    back = lax.dot_general(
        delta_two, weight_two, (((1,), (1,)), ((), ())), preferred_element_type=jnp.float32
    )
    _, pull = jax.vjp(
        lambda grid: build_patches(grid, frames, height, columns),
        jnp.zeros(ext_two.shape, jnp.float32),
    )
    spread = pull(back)[0][:, 1 : height + 1, 1 : columns + 1]
    cache_part = spread[:2]
    own = spread[2:]
    passing = jnp.where(starting, 0.0, cache_part)
    from_next = passed_along(passing.astype(jnp.bfloat16), "tm", -1).astype(passing.dtype)
    own = own.at[frames - 2 :].add(from_next)
    own = own.at[0].add(jnp.where(starting, cache_part[0] + cache_part[1], 0.0))
    delta_one = (own * live * silu_slope(first_act)).astype(jnp.bfloat16).reshape(-1, width)
    count = patches_one.shape[1] // lax.axis_size("space")
    share_one = lax.dynamic_slice_in_dim(patches_one, space * count, count, 1)
    share_two = lax.dynamic_slice_in_dim(patches_two, space * count, count, 1)
    part = jnp.stack([contract(share_one, delta_one), contract(share_two, delta_two)])
    grad_one, grad_two = reduced(part, scale)
    return (output[None], grad_one, grad_two)


def solution(mesh):
    placed = (
        P("tm", None, "space", None, None),
        P("tm", None, "space", None, None),
        P(),
        P(),
        P("tm"),
        P("tm"),
    )
    return jax.shard_map(
        per_device,
        mesh=mesh,
        in_specs=placed,
        out_specs=(P("tm", None, "space", None, None), P("space", None), P("space", None)),
        check_vma=False,
    )
```

```python
import math

import jax
import jax.numpy as jnp
from jax import lax
from jax.experimental import pallas as pl
from jax.experimental.pallas import tpu as pltpu
from jax.sharding import PartitionSpec as P

MESH = pl.DeviceIdType.MESH
HALF = jnp.bfloat16
FULL = jnp.float32
SIDE = 8
SPACE = 4
BLOCK = 112
FRAMES = 8
ROWS = 8
LOW = 2
COLS = 16
WIDTH = 128
PLANE = ROWS * COLS
SHARE = 864


def shifted(value, step):
    rows = value.shape[0]
    column = lax.rem(lax.broadcasted_iota(jnp.int32, value.shape, 0), COLS)
    edge = 0 if step == 1 else COLS - 1
    return jnp.where(column == edge, 0.0, pltpu.roll(value, step % rows, 0))


def joined(wide):
    left, middle, right = wide[:, :WIDTH], wide[:, WIDTH : 2 * WIDTH], wide[:, 2 * WIDTH :]
    return middle + shifted(left, 1) + shifted(right, -1)


def windows(ref, frames, start, height):
    return jnp.concatenate(
        [
            ref[kt : kt + frames, pl.ds(start + kh, height)].reshape(-1, WIDTH)
            for kt in range(3)
            for kh in range(3)
        ],
        axis=1,
    )


def forward_weight(ref):
    return jnp.concatenate(
        [
            jnp.concatenate(
                [ref[(3 * k + kw) * WIDTH : (3 * k + kw + 1) * WIDTH] for k in range(9)], axis=0
            )
            for kw in range(3)
        ],
        axis=1,
    )


def backward_weight(ref):
    return jnp.concatenate(
        [
            jnp.concatenate(
                [
                    ref[(26 - 3 * k - kw) * WIDTH : (27 - 3 * k - kw) * WIDTH]
                    for k in range(9)
                ],
                axis=1,
            )
            for kw in range(3)
        ],
        axis=0,
    )


def kernel(
    scale, video_ref, cotangent_ref, weight_one_ref, weight_two_ref, before_ref, count_ref,
    output_ref, one_ref, two_ref,
    first, second, ext_video, ext_delta, ext_hidden, cache, own_delta, next_delta, act, deltas,
    part, swap_out, swap_in, total, stage, land_a, land_b, wide, other,
    load, v_send, v_recv, vh_send, vh_recv, d_send, d_recv, dh_send, dh_recv, h_send, h_recv,
    swap_send, swap_recv, a_send, a_recv, b_send, b_recv, w_send, w_recv, o_send, o_recv,
):
    tm = lax.axis_index("tm")
    space = lax.axis_index("space")
    groups = 2 * SIDE * SIDE
    core = lax.rem(tm, 2)
    chip = tm // 2
    y, z = chip // SIDE, lax.rem(chip, SIDE)
    a = y * (1 - core) + z * core
    b = z * (1 - core) + y * core
    stride_a, stride_b = 8 - 7 * core, 1 + 7 * core

    def along_a(step):
        at = lax.rem(a + step, SIDE)
        return at, (2 * (at * stride_a + b * stride_b) + core, space)

    def along_b(step):
        at = lax.rem(b + step, SIDE)
        return at, (2 * (a * stride_a + at * stride_b) + core, space)

    def beside(step):
        return (tm, lax.rem(space + step, SPACE))

    def later(step):
        return (lax.rem(tm + 1, groups), lax.rem(space + step, SPACE))

    def earlier(step):
        return (lax.rem(tm + groups - 1, groups), lax.rem(space + step, SPACE))

    sibling = (tm + 1 - 2 * core, space)

    barrier = pltpu.get_barrier_semaphore()
    peers = [beside(step) for step in range(1, SPACE)]
    peers += [later(step) for step in range(SPACE)] + [earlier(step) for step in range(SPACE)]
    peers += [along_a(step)[1] for step in range(1, SIDE)]
    peers += [along_b(step)[1] for step in range(1, SIDE)]
    for device in peers:
        pl.semaphore_signal(barrier, inc=1, device_id=device, device_id_type=MESH)

    loads = [
        pltpu.make_async_copy(weight_one_ref, first, load.at[0]),
        pltpu.make_async_copy(weight_two_ref, second, load.at[1]),
    ]
    for copy in loads:
        copy.start()
    starting = before_ref[0] < 0
    live = [jnp.where(count_ref[0] > frame, 1.0, 0.0) for frame in range(FRAMES)]
    going = jnp.where(starting, 0.0, 1.0)
    for frame in range(FRAMES):
        masked = (live[frame] * cotangent_ref[0, frame].astype(FULL)).astype(HALF)
        own_delta[frame] = masked
        ext_delta[2 + frame, pl.ds(1 + LOW * space, LOW)] = masked
        if frame < 2:
            next_delta[frame] = (going * masked.astype(FULL)).astype(HALF)
    blank = jnp.zeros((COLS, WIDTH), HALF)
    for ref, frames in ((ext_video, 10), (ext_delta, 12), (ext_hidden, 10)):
        for frame in range(frames):
            ref[frame, 0] = blank
            ref[frame, ROWS + 1] = blank
    ext_delta[0:2] = jnp.zeros((2, ROWS + 2, COLS, WIDTH), HALF)
    ext_video[2:, pl.ds(1 + LOW * space, LOW)] = video_ref[0]
    pl.semaphore_wait(barrier, len(peers))

    sent = []

    def send(source, target, send_sem, recv_sem, device):
        copy = pltpu.make_async_remote_copy(
            src_ref=source, dst_ref=target, send_sem=send_sem, recv_sem=recv_sem,
            device_id=device, device_id_type=MESH,
        )
        copy.start()
        sent.append(copy)
        return copy

    place = pl.ds(1 + LOW * space, LOW)
    videos = [
        send(
            video_ref.at[0], ext_video.at[pl.ds(2, FRAMES), place],
            v_send.at[step - 1], v_recv.at[step - 1], beside(step),
        )
        for step in range(1, SPACE)
    ]
    videos += [
        send(
            video_ref.at[0, pl.ds(FRAMES - 2, 2)], ext_video.at[pl.ds(0, 2), place],
            vh_send.at[step], vh_recv.at[step], later(step),
        )
        for step in range(SPACE)
    ]
    changes = [
        send(
            own_delta, ext_delta.at[pl.ds(2, FRAMES), place],
            d_send.at[step - 1], d_recv.at[step - 1], beside(step),
        )
        for step in range(1, SPACE)
    ]
    changes += [
        send(
            next_delta, ext_delta.at[pl.ds(2 + FRAMES, 2), place],
            dh_send.at[step], dh_recv.at[step], earlier(step),
        )
        for step in range(SPACE)
    ]
    for copy in loads:
        copy.wait()
    for copy in videos:
        copy.wait_recv()
    for frame in range(2):
        ext_video[frame] = jnp.where(starting, ext_video[2], ext_video[frame])

    act[...] = joined(
        jnp.dot(
            windows(ext_video, FRAMES, 0, ROWS), forward_weight(first),
            preferred_element_type=FULL,
        )
    )
    for frame in range(FRAMES):
        value = act[frame * PLANE : (frame + 1) * PLANE]
        hidden = (live[frame] * (value * jax.nn.sigmoid(value))).astype(HALF)
        ext_hidden[2 + frame, 1 : 1 + ROWS] = hidden.reshape(ROWS, COLS, WIDTH)
    passing = send(
        ext_hidden.at[pl.ds(FRAMES, 2), pl.ds(1, ROWS)], cache, h_send, h_recv, later(0)
    )

    for copy in changes:
        copy.wait_recv()
    spread = joined(
        lax.dot_general(
            windows(ext_delta, FRAMES + 2, 0, ROWS), backward_weight(second),
            (((1,), (1,)), ((), ())), preferred_element_type=FULL,
        )
    )

    def put(slot, frame, value):
        at = slice(frame * PLANE, (frame + 1) * PLANE)
        deltas[slot, at, 0:WIDTH] = shifted(value, -1).astype(HALF)
        deltas[slot, at, WIDTH : 2 * WIDTH] = value.astype(HALF)
        deltas[slot, at, 2 * WIDTH :] = shifted(value, 1).astype(HALF)

    for frame in range(FRAMES):
        own = spread[(frame + 2) * PLANE : (frame + 3) * PLANE]
        if frame == 0:
            own = own + jnp.where(starting, spread[0:PLANE] + spread[PLANE : 2 * PLANE], 0.0)
        value = act[frame * PLANE : (frame + 1) * PLANE]
        sigma = jax.nn.sigmoid(value)
        put(0, frame, own * live[frame] * (sigma * (1.0 + value * (1.0 - sigma))))

    def gradient(slot, ref):
        pieces = []
        for step in range(3):
            pair = 2 * space + step
            pieces.append(
                ref[pl.ds(pair // 3, FRAMES), pl.ds(lax.rem(pair, 3), ROWS)].reshape(-1, WIDTH)
            )
        term = lax.dot_general(
            jnp.concatenate(pieces, axis=1), deltas[slot],
            (((0,), (0,)), ((), ())), preferred_element_type=FULL,
        )
        for step in range(3):
            for kw in range(3):
                at = (3 * step + kw) * WIDTH
                part[slot, at : at + WIDTH] = term[
                    step * WIDTH : (step + 1) * WIDTH, kw * WIDTH : (kw + 1) * WIDTH
                ]

    share = pl.ds(pl.multiple_of(96 * space, 32), SHARE)
    swap = pltpu.make_async_remote_copy(
        src_ref=swap_out, dst_ref=swap_in, send_sem=swap_send, recv_sem=swap_recv,
        device_id=sibling, device_id_type=MESH,
    )
    gradient(0, ext_video)

    @pl.when(core == 1)
    def _():
        swap_out[...] = part[0, share].astype(HALF)
        swap.start()

    for frame in range(FRAMES):
        put(1, frame, ext_delta[2 + frame, 1 : 1 + ROWS].reshape(PLANE, WIDTH).astype(FULL))
    passing.wait_recv()
    for frame in range(2):
        ext_hidden[frame, 1 : 1 + ROWS] = jnp.where(
            starting, ext_hidden[2, 1 : 1 + ROWS], cache[frame]
        )
    gradient(1, ext_hidden)

    @pl.when(core == 0)
    def _():
        swap_out[...] = part[1, share].astype(HALF)
        swap.start()

    swap.wait_recv()
    total[0:SHARE] = part[core, share] + swap_in[...].astype(FULL)
    total[SHARE:] = jnp.zeros((SIDE * BLOCK - SHARE, WIDTH), FULL)
    stage[...] = total[...].astype(HALF).reshape(stage.shape)
    over_a = []
    for step in range(1, SIDE):
        at, device = along_a(step)
        over_a.append(
            send(stage.at[at], land_a.at[step - 1], a_send.at[step - 1], a_recv.at[step - 1], device)
        )

    result = joined(
        jnp.dot(
            windows(ext_hidden, FRAMES, LOW * space, LOW), forward_weight(second),
            preferred_element_type=FULL,
        )
    ).reshape(FRAMES, LOW * COLS, WIDTH)
    for frame in range(FRAMES):
        value = video_ref[0, frame].reshape(LOW * COLS, WIDTH).astype(FULL) + result[frame]
        output_ref[0, frame] = (live[frame] * value).astype(HALF).reshape(LOW, COLS, WIDTH)

    block = total[pl.ds(pl.multiple_of(a * BLOCK, BLOCK), BLOCK)]
    for step in range(1, SIDE):
        over_a[step - 1].wait_recv()
        block = block + land_a[step - 1].astype(FULL)
    land_b[b] = block.astype(HALF)
    over_b = []
    for step in range(1, SIDE):
        over_b.append(
            send(
                land_b.at[b], land_b.at[b],
                b_send.at[step - 1], b_recv.at[step - 1], along_b(step)[1],
            )
        )
    for copy in over_b:
        copy.wait_recv()
    block = land_b[0].astype(FULL)
    for at in range(1, SIDE):
        block = block + land_b[at].astype(FULL)
    wide[a] = (block * scale).astype(HALF)
    back = []
    for step in range(1, SIDE):
        back.append(
            send(
                wide.at[a], wide.at[a],
                w_send.at[step - 1], w_recv.at[step - 1], along_a(step)[1],
            )
        )
    across = [send(wide.at[a], other.at[a], o_send.at[0], o_recv.at[0], sibling)]
    for step in range(1, SIDE):
        back[step - 1].wait_recv()
        origin = lax.rem(a + SIDE - step, SIDE)
        across.append(
            send(wide.at[origin], other.at[origin], o_send.at[step], o_recv.at[step], sibling)
        )
    for copy in across:
        copy.wait_recv()
    one_ref[...] = jnp.where(core == 0, wide[...], other[...])
    two_ref[...] = jnp.where(core == 0, other[...], wide[...])
    swap.wait_send()
    for copy in sent:
        copy.wait_send()


def per_device(video, cotangent, weight_one, weight_two, predecessor, frame_count):
    frames, height, columns, width = video.shape[1:]
    groups, parts = lax.axis_size("tm"), lax.axis_size("space")
    scale = 1.0 / math.sqrt(groups * parts * frames * height * columns)
    vmem = pl.BlockSpec(memory_space=pltpu.VMEM)
    smem = pl.BlockSpec(memory_space=pltpu.SMEM)
    anywhere = pl.BlockSpec(memory_space=pl.ANY)
    dma = pltpu.SemaphoreType.DMA
    taps = weight_one.shape[0]
    blocks = (SIDE, BLOCK, WIDTH)
    output, one, two = pl.pallas_call(
        lambda *refs: kernel(scale, *refs),
        out_shape=(
            jax.ShapeDtypeStruct(video.shape, HALF),
            jax.ShapeDtypeStruct(blocks, HALF),
            jax.ShapeDtypeStruct(blocks, HALF),
        ),
        in_specs=[vmem, vmem, anywhere, anywhere, smem, smem],
        out_specs=(vmem, vmem, vmem),
        scratch_shapes=[
            pltpu.VMEM((taps, WIDTH), HALF),
            pltpu.VMEM((taps, WIDTH), HALF),
            pltpu.VMEM((FRAMES + 2, ROWS + 2, COLS, WIDTH), HALF),
            pltpu.VMEM((FRAMES + 4, ROWS + 2, COLS, WIDTH), HALF),
            pltpu.VMEM((FRAMES + 2, ROWS + 2, COLS, WIDTH), HALF),
            pltpu.VMEM((2, ROWS, COLS, WIDTH), HALF),
            pltpu.VMEM((FRAMES, LOW, COLS, WIDTH), HALF),
            pltpu.VMEM((2, LOW, COLS, WIDTH), HALF),
            pltpu.VMEM((FRAMES * PLANE, WIDTH), FULL),
            pltpu.VMEM((2, FRAMES * PLANE, 3 * WIDTH), HALF),
            pltpu.VMEM((2, 9 * WIDTH, WIDTH), FULL),
            pltpu.VMEM((SHARE, WIDTH), HALF),
            pltpu.VMEM((SHARE, WIDTH), HALF),
            pltpu.VMEM((SIDE * BLOCK, WIDTH), FULL),
            pltpu.VMEM(blocks, HALF),
            pltpu.VMEM((SIDE - 1, BLOCK, WIDTH), HALF),
            pltpu.VMEM(blocks, HALF),
            pltpu.VMEM(blocks, HALF),
            pltpu.VMEM(blocks, HALF),
            dma((2,)),
            dma((SPACE - 1,)),
            dma((SPACE - 1,)),
            dma((SPACE,)),
            dma((SPACE,)),
            dma((SPACE - 1,)),
            dma((SPACE - 1,)),
            dma((SPACE,)),
            dma((SPACE,)),
            dma,
            dma,
            dma,
            dma,
            dma((SIDE - 1,)),
            dma((SIDE - 1,)),
            dma((SIDE - 1,)),
            dma((SIDE - 1,)),
            dma((SIDE - 1,)),
            dma((SIDE - 1,)),
            dma((SIDE,)),
            dma((SIDE,)),
        ],
        compiler_params=pltpu.CompilerParams(
            collective_id=0, has_side_effects=True, vmem_limit_bytes=48 * 1024 * 1024
        ),
    )(video, cotangent, weight_one, weight_two, predecessor, frame_count)

    def widened(grad):
        return grad.reshape(-1, WIDTH)[: taps // parts].astype(FULL)

    return (output, widened(one), widened(two))


def solution(mesh):
    placed = (
        P("tm", None, "space", None, None),
        P("tm", None, "space", None, None),
        P(),
        P(),
        P("tm"),
        P("tm"),
    )
    return jax.shard_map(
        per_device,
        mesh=mesh,
        in_specs=placed,
        out_specs=(P("tm", None, "space", None, None), P("space", None), P("space", None)),
        check_vma=False,
    )
```

```python
import math

import jax
import jax.numpy as jnp
from jax import lax
from jax.experimental import pallas as pl
from jax.experimental.pallas import tpu as pltpu
from jax.sharding import PartitionSpec as P

MESH = pl.DeviceIdType.MESH
HALF = jnp.bfloat16
FULL = jnp.float32
SIDE = 8
SPACE = 4
BLOCK = 112
FRAMES = 8
ROWS = 8
LOW = 2
COLS = 16
WIDTH = 128
PLANE = ROWS * COLS
SHARE = 864
TILE = 16
CHUNKS = (pl.ds(0, 64), pl.ds(64, 48))


def shifted(value, step):
    rows = value.shape[0]
    column = lax.rem(lax.broadcasted_iota(jnp.int32, value.shape, 0), COLS)
    edge = 0 if step == 1 else COLS - 1
    return jnp.where(column == edge, 0.0, pltpu.roll(value, step % rows, 0))


def joined(wide):
    left, middle, right = wide[:, :WIDTH], wide[:, WIDTH : 2 * WIDTH], wide[:, 2 * WIDTH :]
    return middle + shifted(left, 1) + shifted(right, -1)


def windows(ref, frames, start, height):
    return jnp.concatenate(
        [
            ref[kt : kt + frames, pl.ds(start + kh, height)].reshape(-1, WIDTH)
            for kt in range(3)
            for kh in range(3)
        ],
        axis=1,
    )


def forward_weight(ref):
    return jnp.concatenate(
        [
            jnp.concatenate(
                [ref[(3 * k + kw) * WIDTH : (3 * k + kw + 1) * WIDTH] for k in range(9)], axis=0
            )
            for kw in range(3)
        ],
        axis=1,
    )


def backward_weight(ref):
    return jnp.concatenate(
        [
            jnp.concatenate(
                [
                    ref[(26 - 3 * k - kw) * WIDTH : (27 - 3 * k - kw) * WIDTH]
                    for k in range(9)
                ],
                axis=1,
            )
            for kw in range(3)
        ],
        axis=0,
    )


def kernel(
    scale, video_ref, cotangent_ref, weight_one_ref, weight_two_ref, before_ref, count_ref,
    output_ref, grads_ref,
    result_out, first, second, own_video, cotangent_in, ext_video, ext_delta, ext_hidden, cache, own_delta, next_delta, act, deltas,
    part, swap_out, swap_in, total, stage, land_a, land_b, wide,
    load, store, v_send, v_recv, vh_send, vh_recv, d_send, d_recv, dh_send, dh_recv, h_send, h_recv,
    swap_send, swap_recv, a_send, a_recv, b_send, b_recv, w_send, w_recv, o_send, o_recv,
):
    tm = lax.axis_index("tm")
    space = lax.axis_index("space")
    groups = 2 * SIDE * SIDE
    core = lax.rem(tm, 2)
    chip = tm // 2
    y, z = chip // SIDE, lax.rem(chip, SIDE)
    a = y * (1 - core) + z * core
    b = z * (1 - core) + y * core
    stride_a, stride_b = 8 - 7 * core, 1 + 7 * core

    def along_a(step):
        at = lax.rem(a + step, SIDE)
        return at, (2 * (at * stride_a + b * stride_b) + core, space)

    def along_b(step):
        at = lax.rem(b + step, SIDE)
        return at, (2 * (a * stride_a + at * stride_b) + core, space)

    def beside(step):
        return (tm, lax.rem(space + step, SPACE))

    def later(step):
        return (lax.rem(tm + 1, groups), lax.rem(space + step, SPACE))

    def earlier(step):
        return (lax.rem(tm + groups - 1, groups), lax.rem(space + step, SPACE))

    sibling = (tm + 1 - 2 * core, space)

    barrier = pltpu.get_barrier_semaphore()
    peers = [beside(step) for step in range(1, SPACE)]
    peers += [later(step) for step in range(SPACE)] + [earlier(step) for step in range(SPACE)]
    peers += [along_a(step)[1] for step in range(1, SIDE)]
    peers += [along_b(step)[1] for step in range(1, SIDE)]
    for device in peers:
        pl.semaphore_signal(barrier, inc=1, device_id=device, device_id_type=MESH)

    loads = [
        pltpu.make_async_copy(weight_one_ref, first, load.at[0]),
        pltpu.make_async_copy(weight_two_ref, second, load.at[1]),
    ]
    video_load = pltpu.make_async_copy(video_ref.at[0], own_video, load.at[2])
    cotangent_load = pltpu.make_async_copy(cotangent_ref.at[0], cotangent_in, load.at[3])
    for copy in [video_load, cotangent_load] + loads:
        copy.start()
    blank = jnp.zeros((COLS, WIDTH), HALF)
    for ref, frames in ((ext_video, 10), (ext_delta, 12), (ext_hidden, 10)):
        for frame in range(frames):
            ref[frame, 0] = blank
            ref[frame, ROWS + 1] = blank
    ext_delta[0:2] = jnp.zeros((2, ROWS + 2, COLS, WIDTH), HALF)
    starting = before_ref[0] < 0
    live = [jnp.where(count_ref[0] > frame, 1.0, 0.0) for frame in range(FRAMES)]
    going = jnp.where(starting, 0.0, 1.0)
    cotangent_load.wait()
    for frame in range(FRAMES):
        masked = (live[frame] * cotangent_in[frame].astype(FULL)).astype(HALF)
        own_delta[frame] = masked
        ext_delta[2 + frame, pl.ds(1 + LOW * space, LOW)] = masked
        if frame < 2:
            next_delta[frame] = (going * masked.astype(FULL)).astype(HALF)
    video_load.wait()
    ext_video[2:, pl.ds(1 + LOW * space, LOW)] = own_video[...]
    pl.semaphore_wait(barrier, len(peers))

    sent = []

    def send(source, target, send_sem, recv_sem, device):
        copy = pltpu.make_async_remote_copy(
            src_ref=source, dst_ref=target, send_sem=send_sem, recv_sem=recv_sem,
            device_id=device, device_id_type=MESH,
        )
        copy.start()
        sent.append(copy)
        return copy

    place = pl.ds(1 + LOW * space, LOW)
    videos = [
        send(
            own_video, ext_video.at[pl.ds(2, FRAMES), place],
            v_send.at[step - 1], v_recv.at[step - 1], beside(step),
        )
        for step in range(1, SPACE)
    ]
    videos += [
        send(
            own_video.at[pl.ds(FRAMES - 2, 2)], ext_video.at[pl.ds(0, 2), place],
            vh_send.at[step], vh_recv.at[step], later(step),
        )
        for step in range(SPACE)
    ]
    changes = [
        send(
            own_delta, ext_delta.at[pl.ds(2, FRAMES), place],
            d_send.at[step - 1], d_recv.at[step - 1], beside(step),
        )
        for step in range(1, SPACE)
    ]
    changes += [
        send(
            next_delta, ext_delta.at[pl.ds(2 + FRAMES, 2), place],
            dh_send.at[step], dh_recv.at[step], earlier(step),
        )
        for step in range(SPACE)
    ]
    for copy in loads:
        copy.wait()
    for copy in videos:
        copy.wait_recv()
    for frame in range(2):
        ext_video[frame] = jnp.where(starting, ext_video[2], ext_video[frame])

    act[...] = joined(
        jnp.dot(
            windows(ext_video, FRAMES, 0, ROWS), forward_weight(first),
            preferred_element_type=FULL,
        )
    )
    for frame in range(FRAMES):
        value = act[frame * PLANE : (frame + 1) * PLANE]
        hidden = (live[frame] * (value * jax.nn.sigmoid(value))).astype(HALF)
        ext_hidden[2 + frame, 1 : 1 + ROWS] = hidden.reshape(ROWS, COLS, WIDTH)
    passing = send(
        ext_hidden.at[pl.ds(FRAMES, 2), pl.ds(1, ROWS)], cache, h_send, h_recv, later(0)
    )

    for copy in changes:
        copy.wait_recv()
    spread = joined(
        lax.dot_general(
            windows(ext_delta, FRAMES + 2, 0, ROWS), backward_weight(second),
            (((1,), (1,)), ((), ())), preferred_element_type=FULL,
        )
    )

    def put(slot, frame, value):
        at = slice(frame * PLANE, (frame + 1) * PLANE)
        deltas[slot, at, 0:WIDTH] = shifted(value, -1).astype(HALF)
        deltas[slot, at, WIDTH : 2 * WIDTH] = value.astype(HALF)
        deltas[slot, at, 2 * WIDTH :] = shifted(value, 1).astype(HALF)

    for frame in range(FRAMES):
        own = spread[(frame + 2) * PLANE : (frame + 3) * PLANE]
        if frame == 0:
            own = own + jnp.where(starting, spread[0:PLANE] + spread[PLANE : 2 * PLANE], 0.0)
        value = act[frame * PLANE : (frame + 1) * PLANE]
        sigma = jax.nn.sigmoid(value)
        put(0, frame, own * live[frame] * (sigma * (1.0 + value * (1.0 - sigma))))

    def gradient(slot, ref):
        pieces = []
        for step in range(3):
            pair = 2 * space + step
            pieces.append(
                ref[pl.ds(pair // 3, FRAMES), pl.ds(lax.rem(pair, 3), ROWS)].reshape(-1, WIDTH)
            )
        term = lax.dot_general(
            jnp.concatenate(pieces, axis=1), deltas[slot],
            (((0,), (0,)), ((), ())), preferred_element_type=FULL,
        )
        for step in range(3):
            for kw in range(3):
                at = (3 * step + kw) * WIDTH
                part[slot, at : at + WIDTH] = term[
                    step * WIDTH : (step + 1) * WIDTH, kw * WIDTH : (kw + 1) * WIDTH
                ]

    share = pl.ds(pl.multiple_of(96 * space, 32), SHARE)
    swap = pltpu.make_async_remote_copy(
        src_ref=swap_out, dst_ref=swap_in, send_sem=swap_send, recv_sem=swap_recv,
        device_id=sibling, device_id_type=MESH,
    )
    gradient(0, ext_video)

    @pl.when(core == 1)
    def _():
        swap_out[...] = part[0, share].astype(HALF)
        swap.start()

    for frame in range(FRAMES):
        put(1, frame, ext_delta[2 + frame, 1 : 1 + ROWS].reshape(PLANE, WIDTH).astype(FULL))
    passing.wait_recv()
    for frame in range(2):
        ext_hidden[frame, 1 : 1 + ROWS] = jnp.where(
            starting, ext_hidden[2, 1 : 1 + ROWS], cache[frame]
        )
    gradient(1, ext_hidden)

    @pl.when(core == 0)
    def _():
        swap_out[...] = part[1, share].astype(HALF)
        swap.start()

    swap.wait_recv()
    total[0:SHARE] = part[core, share] + swap_in[...].astype(FULL)
    total[SHARE:] = jnp.zeros((SIDE * BLOCK - SHARE, WIDTH), FULL)
    stage[...] = total[...].astype(HALF).reshape(stage.shape)
    over_a = []
    for number, chunk in enumerate(CHUNKS):
        for step in range(1, SIDE):
            at, device = along_a(step)
            over_a.append(
                send(
                    stage.at[at, chunk], land_a.at[step - 1, chunk],
                    a_send.at[number, step - 1], a_recv.at[number, step - 1], device,
                )
            )

    result = joined(
        jnp.dot(
            windows(ext_hidden, FRAMES, LOW * space, LOW), forward_weight(second),
            preferred_element_type=FULL,
        )
    ).reshape(FRAMES, LOW * COLS, WIDTH)
    for frame in range(FRAMES):
        value = own_video[frame].reshape(LOW * COLS, WIDTH).astype(FULL) + result[frame]
        result_out[frame] = (live[frame] * value).astype(HALF).reshape(LOW, COLS, WIDTH)
    stores = [pltpu.make_async_copy(result_out, output_ref.at[0], store.at[0])]
    stores[0].start()

    over_b = []
    for number, chunk in enumerate(CHUNKS):
        block = total[pl.ds(pl.multiple_of(a * BLOCK + chunk.start, TILE), chunk.size)]
        for step in range(1, SIDE):
            over_a[(SIDE - 1) * number + step - 1].wait_recv()
            block = block + land_a[step - 1, chunk].astype(FULL)
        land_b[b, chunk] = block.astype(HALF)
        for step in range(1, SIDE):
            over_b.append(
                send(
                    land_b.at[b, chunk], land_b.at[b, chunk],
                    b_send.at[number, step - 1], b_recv.at[number, step - 1], along_b(step)[1],
                )
            )
    back, across = [], []
    for number, chunk in enumerate(CHUNKS):
        for step in range(1, SIDE):
            over_b[(SIDE - 1) * number + step - 1].wait_recv()
        block = land_b[0, chunk].astype(FULL)
        for at in range(1, SIDE):
            block = block + land_b[at, chunk].astype(FULL)
        wide[a, chunk] = (block * scale).astype(HALF)
        for step in range(1, SIDE):
            back.append(
                send(
                    wide.at[a, chunk], wide.at[a, chunk],
                    w_send.at[number, step - 1], w_recv.at[number, step - 1], along_a(step)[1],
                )
            )
        across.append(
            send(
                wide.at[a, chunk], grads_ref.at[core, a, chunk],
                o_send.at[number, 0], o_recv.at[number, 0], sibling,
            )
        )
    for number, chunk in enumerate(CHUNKS):
        for step in range(1, SIDE):
            back[(SIDE - 1) * number + step - 1].wait_recv()
            origin = lax.rem(a + SIDE - step, SIDE)
            across.append(
                send(
                    wide.at[origin, chunk], grads_ref.at[core, origin, chunk],
                    o_send.at[number, step], o_recv.at[number, step], sibling,
                )
            )
    stores.append(pltpu.make_async_copy(wide, grads_ref.at[core], store.at[1]))
    stores[1].start()
    for copy in across:
        copy.wait_recv()
    for copy in stores:
        copy.wait()
    swap.wait_send()
    for copy in sent:
        copy.wait_send()


def per_device(video, cotangent, weight_one, weight_two, predecessor, frame_count):
    frames, height, columns, width = video.shape[1:]
    groups, parts = lax.axis_size("tm"), lax.axis_size("space")
    scale = 1.0 / math.sqrt(groups * parts * frames * height * columns)
    far = pl.BlockSpec(memory_space=pltpu.HBM)
    dma = pltpu.SemaphoreType.DMA
    taps = weight_one.shape[0]
    blocks = (SIDE, BLOCK, WIDTH)
    output, grads = pl.pallas_call(
        lambda *refs: kernel(scale, *refs),
        out_shape=(
            jax.ShapeDtypeStruct(video.shape, HALF),
            jax.ShapeDtypeStruct((2,) + blocks, HALF),
        ),
        in_specs=[far] * 4 + [pl.BlockSpec(memory_space=pltpu.SMEM)] * 2,
        out_specs=(far, far),
        scratch_shapes=[
            pltpu.VMEM((FRAMES, LOW, COLS, WIDTH), HALF),
            pltpu.VMEM((taps, WIDTH), HALF),
            pltpu.VMEM((taps, WIDTH), HALF),
            pltpu.VMEM((FRAMES, LOW, COLS, WIDTH), HALF),
            pltpu.VMEM((FRAMES, LOW, COLS, WIDTH), HALF),
            pltpu.VMEM((FRAMES + 2, ROWS + 2, COLS, WIDTH), HALF),
            pltpu.VMEM((FRAMES + 4, ROWS + 2, COLS, WIDTH), HALF),
            pltpu.VMEM((FRAMES + 2, ROWS + 2, COLS, WIDTH), HALF),
            pltpu.VMEM((2, ROWS, COLS, WIDTH), HALF),
            pltpu.VMEM((FRAMES, LOW, COLS, WIDTH), HALF),
            pltpu.VMEM((2, LOW, COLS, WIDTH), HALF),
            pltpu.VMEM((FRAMES * PLANE, WIDTH), FULL),
            pltpu.VMEM((2, FRAMES * PLANE, 3 * WIDTH), HALF),
            pltpu.VMEM((2, 9 * WIDTH, WIDTH), FULL),
            pltpu.VMEM((SHARE, WIDTH), HALF),
            pltpu.VMEM((SHARE, WIDTH), HALF),
            pltpu.VMEM((SIDE * BLOCK, WIDTH), FULL),
            pltpu.VMEM(blocks, HALF),
            pltpu.VMEM((SIDE - 1, BLOCK, WIDTH), HALF),
            pltpu.VMEM(blocks, HALF),
            pltpu.VMEM(blocks, HALF),
            dma((4,)),
            dma((2,)),
            dma((SPACE - 1,)),
            dma((SPACE - 1,)),
            dma((SPACE,)),
            dma((SPACE,)),
            dma((SPACE - 1,)),
            dma((SPACE - 1,)),
            dma((SPACE,)),
            dma((SPACE,)),
            dma,
            dma,
            dma,
            dma,
            dma((len(CHUNKS), SIDE - 1)),
            dma((len(CHUNKS), SIDE - 1)),
            dma((len(CHUNKS), SIDE - 1)),
            dma((len(CHUNKS), SIDE - 1)),
            dma((len(CHUNKS), SIDE - 1)),
            dma((len(CHUNKS), SIDE - 1)),
            dma((len(CHUNKS), SIDE)),
            dma((len(CHUNKS), SIDE)),
        ],
        compiler_params=pltpu.CompilerParams(
            collective_id=0, has_side_effects=True, vmem_limit_bytes=62 * 1024 * 1024
        ),
    )(video, cotangent, weight_one, weight_two, predecessor, frame_count)

    flat = grads.reshape(-1, WIDTH)

    def widened(number):
        begin = number * SIDE * BLOCK
        return flat[begin : begin + taps // parts].astype(FULL)

    return (output, widened(0), widened(1))


def solution(mesh):
    placed = (
        P("tm", None, "space", None, None),
        P("tm", None, "space", None, None),
        P(),
        P(),
        P("tm"),
        P("tm"),
    )
    return jax.shard_map(
        per_device,
        mesh=mesh,
        in_specs=placed,
        out_specs=(P("tm", None, "space", None, None), P("space", None), P("space", None)),
        check_vma=False,
    )
```

```python
import math

import jax
import jax.numpy as jnp
from jax import lax
from jax.experimental import pallas as pl
from jax.experimental.pallas import tpu as pltpu
from jax.sharding import PartitionSpec as P

MESH = pl.DeviceIdType.MESH
HALF = jnp.bfloat16
FULL = jnp.float32
SIDE = 8
SPACE = 4
BLOCK = 112
FRAMES = 8
ROWS = 8
LOW = 2
COLS = 16
WIDTH = 128
PLANE = ROWS * COLS
SHARE = 864
TILE = 16
CHUNKS = (pl.ds(0, 64), pl.ds(64, 48))


def shifted(value, step):
    rows = value.shape[0]
    column = lax.rem(lax.broadcasted_iota(jnp.int32, value.shape, 0), COLS)
    edge = 0 if step == 1 else COLS - 1
    return jnp.where(column == edge, 0.0, pltpu.roll(value, step % rows, 0))


def joined(wide):
    left, middle, right = wide[:, :WIDTH], wide[:, WIDTH : 2 * WIDTH], wide[:, 2 * WIDTH :]
    return middle + shifted(left, 1) + shifted(right, -1)


def windows(ref, frames, start, height):
    return jnp.concatenate(
        [
            ref[kt : kt + frames, pl.ds(start + kh, height)].reshape(-1, WIDTH)
            for kt in range(3)
            for kh in range(3)
        ],
        axis=1,
    )


def forward_weight(ref):
    return jnp.concatenate(
        [
            jnp.concatenate(
                [ref[(3 * k + kw) * WIDTH : (3 * k + kw + 1) * WIDTH] for k in range(9)], axis=0
            )
            for kw in range(3)
        ],
        axis=1,
    )


def backward_weight(ref):
    return jnp.concatenate(
        [
            jnp.concatenate(
                [
                    ref[(26 - 3 * k - kw) * WIDTH : (27 - 3 * k - kw) * WIDTH]
                    for k in range(9)
                ],
                axis=1,
            )
            for kw in range(3)
        ],
        axis=0,
    )


def kernel(
    scale, video_ref, cotangent_ref, weight_one_ref, weight_two_ref, before_ref, count_ref,
    output_ref, grads_ref,
    result_out, first, second, own_video, cotangent_in, ext_both, ext_delta, cache, own_delta, next_delta, slope, deltas,
    part, swap_out, swap_in, total, stage, land_a, land_b, wide,
    load, store, v_send, v_recv, vh_send, vh_recv, d_send, d_recv, dh_send, dh_recv, h_send, h_recv,
    swap_send, swap_recv, a_send, a_recv, b_send, b_recv, w_send, w_recv, o_send, o_recv,
):
    tm = lax.axis_index("tm")
    space = lax.axis_index("space")
    groups = 2 * SIDE * SIDE
    core = lax.rem(tm, 2)
    chip = tm // 2
    y, z = chip // SIDE, lax.rem(chip, SIDE)
    a = y * (1 - core) + z * core
    b = z * (1 - core) + y * core
    stride_a, stride_b = 8 - 7 * core, 1 + 7 * core

    def along_a(step):
        at = lax.rem(a + step, SIDE)
        return at, (2 * (at * stride_a + b * stride_b) + core, space)

    def along_b(step):
        at = lax.rem(b + step, SIDE)
        return at, (2 * (a * stride_a + at * stride_b) + core, space)

    def beside(step):
        return (tm, lax.rem(space + step, SPACE))

    def later(step):
        return (lax.rem(tm + 1, groups), lax.rem(space + step, SPACE))

    def earlier(step):
        return (lax.rem(tm + groups - 1, groups), lax.rem(space + step, SPACE))

    sibling = (tm + 1 - 2 * core, space)

    barrier = pltpu.get_barrier_semaphore()
    near = [beside(step) for step in range(1, SPACE)]
    near += [later(step) for step in range(SPACE)] + [earlier(step) for step in range(SPACE)]
    distant = [along_a(step)[1] for step in range(1, SIDE)]
    distant += [along_b(step)[1] for step in range(1, SIDE)]
    for device in near:
        pl.semaphore_signal(barrier, inc=1, device_id=device, device_id_type=MESH)
    loads = [
        pltpu.make_async_copy(weight_one_ref, first, load.at[0]),
        pltpu.make_async_copy(weight_two_ref, second, load.at[1]),
    ]
    video_load = pltpu.make_async_copy(video_ref.at[0], own_video, load.at[2])
    cotangent_load = pltpu.make_async_copy(cotangent_ref.at[0], cotangent_in, load.at[3])
    for copy in [video_load, cotangent_load] + loads:
        copy.start()
    for device in distant:
        pl.semaphore_signal(barrier, inc=1, device_id=device, device_id_type=MESH)

    ext_video, ext_hidden = ext_both.at[0], ext_both.at[1]
    blank = jnp.zeros((COLS, WIDTH), HALF)
    for ref, frames in ((ext_video, 10), (ext_delta, 12), (ext_hidden, 10)):
        for frame in range(frames):
            ref[frame, 0] = blank
            ref[frame, ROWS + 1] = blank
    ext_delta[0:2] = jnp.zeros((2, ROWS + 2, COLS, WIDTH), HALF)
    starting = before_ref[0] < 0
    live = [jnp.where(count_ref[0] > frame, 1.0, 0.0) for frame in range(FRAMES)]
    going = jnp.where(starting, 0.0, 1.0)
    cotangent_load.wait()
    for frame in range(FRAMES):
        masked = (live[frame] * cotangent_in[frame].astype(FULL)).astype(HALF)
        own_delta[frame] = masked
        ext_delta[2 + frame, pl.ds(1 + LOW * space, LOW)] = masked
        if frame < 2:
            next_delta[frame] = (going * masked.astype(FULL)).astype(HALF)
    video_load.wait()
    ext_video[2:, pl.ds(1 + LOW * space, LOW)] = own_video[...]
    pl.semaphore_wait(barrier, len(near) + len(distant))

    def send(source, target, send_sem, recv_sem, device):
        copy = pltpu.make_async_remote_copy(
            src_ref=source, dst_ref=target, send_sem=send_sem, recv_sem=recv_sem,
            device_id=device, device_id_type=MESH,
        )
        copy.start()
        return copy

    place = pl.ds(1 + LOW * space, LOW)
    videos = [
        send(
            own_video, ext_video.at[pl.ds(2, FRAMES), place],
            v_send.at[step - 1], v_recv.at[step - 1], beside(step),
        )
        for step in range(1, SPACE)
    ]
    videos += [
        send(
            own_video.at[pl.ds(FRAMES - 2, 2)], ext_video.at[pl.ds(0, 2), place],
            vh_send.at[step], vh_recv.at[step], later(step),
        )
        for step in range(SPACE)
    ]
    changes = [
        send(
            own_delta, ext_delta.at[pl.ds(2, FRAMES), place],
            d_send.at[step - 1], d_recv.at[step - 1], beside(step),
        )
        for step in range(1, SPACE)
    ]
    changes += [
        send(
            next_delta, ext_delta.at[pl.ds(2 + FRAMES, 2), place],
            dh_send.at[step], dh_recv.at[step], earlier(step),
        )
        for step in range(SPACE)
    ]
    for copy in loads:
        copy.wait()
    for copy in videos:
        copy.wait_recv()
    for frame in range(2):
        ext_video[frame] = jnp.where(starting, ext_video[2], ext_video[frame])

    act = joined(
        jnp.dot(
            windows(ext_video, FRAMES, 0, ROWS), forward_weight(first),
            preferred_element_type=FULL,
        )
    )
    for frame in range(FRAMES):
        value = act[frame * PLANE : (frame + 1) * PLANE]
        sigma = jax.nn.sigmoid(value)
        hidden = (live[frame] * (value * sigma)).astype(HALF)
        slope[frame * PLANE : (frame + 1) * PLANE] = live[frame] * (
            sigma * (1.0 + value * (1.0 - sigma))
        )
        ext_hidden[2 + frame, 1 : 1 + ROWS] = hidden.reshape(ROWS, COLS, WIDTH)
    passing = send(
        ext_hidden.at[pl.ds(FRAMES, 2), pl.ds(1, ROWS)], cache, h_send, h_recv, later(0)
    )

    for copy in changes:
        copy.wait_recv()
    spread = joined(
        lax.dot_general(
            windows(ext_delta, FRAMES + 2, 0, ROWS), backward_weight(second),
            (((1,), (1,)), ((), ())), preferred_element_type=FULL,
        )
    )

    def put(slot, frame, value):
        at = slice(frame * PLANE, (frame + 1) * PLANE)
        deltas[slot, at, 0:WIDTH] = shifted(value, -1).astype(HALF)
        deltas[slot, at, WIDTH : 2 * WIDTH] = value.astype(HALF)
        deltas[slot, at, 2 * WIDTH :] = shifted(value, 1).astype(HALF)

    for frame in range(FRAMES):
        own = spread[(frame + 2) * PLANE : (frame + 3) * PLANE]
        if frame == 0:
            own = own + jnp.where(starting, spread[0:PLANE] + spread[PLANE : 2 * PLANE], 0.0)
        put(0, frame, own * slope[frame * PLANE : (frame + 1) * PLANE])

    for frame in range(FRAMES):
        put(1, frame, ext_delta[2 + frame, 1 : 1 + ROWS].reshape(PLANE, WIDTH).astype(FULL))
    passing.wait_recv()
    for frame in range(2):
        ext_hidden[frame, 1 : 1 + ROWS] = jnp.where(
            starting, ext_hidden[2, 1 : 1 + ROWS], cache[frame]
        )

    def gradient(slot):
        pieces = []
        for step in range(3):
            pair = 2 * space + step
            piece = ext_both[slot, pl.ds(pair // 3, FRAMES), pl.ds(lax.rem(pair, 3), ROWS)]
            pieces.append(piece.reshape(-1, WIDTH))
        term = lax.dot_general(
            jnp.concatenate(pieces, axis=1), deltas[slot],
            (((0,), (0,)), ((), ())), preferred_element_type=FULL,
        )
        for step in range(3):
            for kw in range(3):
                at = (3 * step + kw) * WIDTH
                part[at : at + WIDTH] = term[
                    step * WIDTH : (step + 1) * WIDTH, kw * WIDTH : (kw + 1) * WIDTH
                ]
        return part[pl.ds(pl.multiple_of(96 * space, 32), SHARE)]

    swap_out[...] = gradient(1 - core).astype(HALF)
    swap = send(swap_out, swap_in, swap_send, swap_recv, sibling)
    total[0:SHARE] = gradient(core)
    total[SHARE:] = jnp.zeros((SIDE * BLOCK - SHARE, WIDTH), FULL)
    swap.wait_recv()
    total[0:SHARE] += swap_in[...].astype(FULL)
    stage[...] = total[...].astype(HALF).reshape(stage.shape)

    def phase(number, chunk, source, target, send_sem, recv_sem, along):
        for step in range(1, SIDE):
            at, device = along(step)
            send(
                source(at), target(step), send_sem.at[number], recv_sem.at[number], device
            )
        seven = land_a.at[pl.ds(0, SIDE - 1), chunk]
        return (
            pltpu.make_async_copy(seven, seven, send_sem.at[number]),
            pltpu.make_async_copy(seven, seven, recv_sem.at[number]),
        )

    over_a = [
        phase(
            number, chunk, lambda at: stage.at[at, chunk], lambda step: land_a.at[step - 1, chunk],
            a_send, a_recv, along_a,
        )
        for number, chunk in enumerate(CHUNKS)
    ]
    for copy in videos + changes + [passing, swap]:
        copy.wait_send()

    result = joined(
        jnp.dot(
            windows(ext_hidden, FRAMES, LOW * space, LOW), forward_weight(second),
            preferred_element_type=FULL,
        )
    ).reshape(FRAMES, LOW * COLS, WIDTH)
    for frame in range(FRAMES):
        value = own_video[frame].reshape(LOW * COLS, WIDTH).astype(FULL) + result[frame]
        result_out[frame] = (live[frame] * value).astype(HALF).reshape(LOW, COLS, WIDTH)
    stores = [pltpu.make_async_copy(result_out, output_ref.at[0], store.at[0])]
    stores[0].start()

    over_b = []
    for number, chunk in enumerate(CHUNKS):
        block = total[pl.ds(pl.multiple_of(a * BLOCK + chunk.start, TILE), chunk.size)]
        over_a[number][1].wait()
        for step in range(1, SIDE):
            block = block + land_a[step - 1, chunk].astype(FULL)
        land_b[b, chunk] = block.astype(HALF)
        over_b.append(
            phase(
                number, chunk, lambda at: land_b.at[b, chunk], lambda step: land_b.at[b, chunk],
                b_send, b_recv, along_b,
            )
        )
    for copy, _ in over_a:
        copy.wait()
    back, across = [], []
    for number, chunk in enumerate(CHUNKS):
        over_b[number][1].wait()
        block = land_b[0, chunk].astype(FULL)
        for at in range(1, SIDE):
            block = block + land_b[at, chunk].astype(FULL)
        wide[a, chunk] = (block * scale).astype(HALF)
        for step in range(1, SIDE):
            back.append(
                send(
                    wide.at[a, chunk], wide.at[a, chunk],
                    w_send.at[number, step - 1], w_recv.at[number, step - 1], along_a(step)[1],
                )
            )
        across.append(
            send(
                wide.at[a, chunk], grads_ref.at[core, a, chunk],
                o_send.at[number, 0], o_recv.at[number, 0], sibling,
            )
        )
    for copy, _ in over_b:
        copy.wait()
    for number, chunk in enumerate(CHUNKS):
        for step in range(1, SIDE):
            back[(SIDE - 1) * number + step - 1].wait_recv()
            origin = lax.rem(a + SIDE - step, SIDE)
            across.append(
                send(
                    wide.at[origin, chunk], grads_ref.at[core, origin, chunk],
                    o_send.at[number, step], o_recv.at[number, step], sibling,
                )
            )
    stores.append(pltpu.make_async_copy(wide, grads_ref.at[core], store.at[1]))
    stores[1].start()
    for copy in back:
        copy.wait_send()
    for copy in across:
        copy.wait()
    for copy in stores:
        copy.wait()


def per_device(video, cotangent, weight_one, weight_two, predecessor, frame_count):
    frames, height, columns, width = video.shape[1:]
    groups, parts = lax.axis_size("tm"), lax.axis_size("space")
    scale = 1.0 / math.sqrt(groups * parts * frames * height * columns)
    far = pl.BlockSpec(memory_space=pltpu.HBM)
    dma = pltpu.SemaphoreType.DMA
    taps = weight_one.shape[0]
    blocks = (SIDE, BLOCK, WIDTH)
    output, grads = pl.pallas_call(
        lambda *refs: kernel(scale, *refs),
        out_shape=(
            jax.ShapeDtypeStruct(video.shape, HALF),
            jax.ShapeDtypeStruct((2,) + blocks, HALF),
        ),
        in_specs=[far] * 4 + [pl.BlockSpec(memory_space=pltpu.SMEM)] * 2,
        out_specs=(far, far),
        scratch_shapes=[
            pltpu.VMEM((FRAMES, LOW, COLS, WIDTH), HALF),
            pltpu.VMEM((taps, WIDTH), HALF),
            pltpu.VMEM((taps, WIDTH), HALF),
            pltpu.VMEM((FRAMES, LOW, COLS, WIDTH), HALF),
            pltpu.VMEM((FRAMES, LOW, COLS, WIDTH), HALF),
            pltpu.VMEM((2, FRAMES + 2, ROWS + 2, COLS, WIDTH), HALF),
            pltpu.VMEM((FRAMES + 4, ROWS + 2, COLS, WIDTH), HALF),
            pltpu.VMEM((2, ROWS, COLS, WIDTH), HALF),
            pltpu.VMEM((FRAMES, LOW, COLS, WIDTH), HALF),
            pltpu.VMEM((2, LOW, COLS, WIDTH), HALF),
            pltpu.VMEM((FRAMES * PLANE, WIDTH), FULL),
            pltpu.VMEM((2, FRAMES * PLANE, 3 * WIDTH), HALF),
            pltpu.VMEM((9 * WIDTH, WIDTH), FULL),
            pltpu.VMEM((SHARE, WIDTH), HALF),
            pltpu.VMEM((SHARE, WIDTH), HALF),
            pltpu.VMEM((SIDE * BLOCK, WIDTH), FULL),
            pltpu.VMEM(blocks, HALF),
            pltpu.VMEM((SIDE - 1, BLOCK, WIDTH), HALF),
            pltpu.VMEM(blocks, HALF),
            pltpu.VMEM(blocks, HALF),
            dma((4,)),
            dma((2,)),
            dma((SPACE - 1,)),
            dma((SPACE - 1,)),
            dma((SPACE,)),
            dma((SPACE,)),
            dma((SPACE - 1,)),
            dma((SPACE - 1,)),
            dma((SPACE,)),
            dma((SPACE,)),
            dma,
            dma,
            dma,
            dma,
            dma((len(CHUNKS),)),
            dma((len(CHUNKS),)),
            dma((len(CHUNKS),)),
            dma((len(CHUNKS),)),
            dma((len(CHUNKS), SIDE - 1)),
            dma((len(CHUNKS), SIDE - 1)),
            dma((len(CHUNKS), SIDE)),
            dma((len(CHUNKS), SIDE)),
        ],
        compiler_params=pltpu.CompilerParams(
            collective_id=0, has_side_effects=True, vmem_limit_bytes=62 * 1024 * 1024
        ),
    )(video, cotangent, weight_one, weight_two, predecessor, frame_count)

    flat = grads.reshape(-1, WIDTH)

    def widened(number):
        begin = number * SIDE * BLOCK
        return flat[begin : begin + taps // parts].astype(FULL)

    return (output, widened(0), widened(1))


def solution(mesh):
    placed = (
        P("tm", None, "space", None, None),
        P("tm", None, "space", None, None),
        P(),
        P(),
        P("tm"),
        P("tm"),
    )
    return jax.shard_map(
        per_device,
        mesh=mesh,
        in_specs=placed,
        out_specs=(P("tm", None, "space", None, None), P("space", None), P("space", None)),
        check_vma=False,
    )
```

```python
import math

import jax
import jax.numpy as jnp
from jax import lax
from jax.experimental import pallas as pl
from jax.experimental.pallas import tpu as pltpu
from jax.sharding import PartitionSpec as P

MESH = pl.DeviceIdType.MESH
HALF = jnp.bfloat16
FULL = jnp.float32
SIDE = 8
SPACE = 4
BLOCK = 112
FRAMES = 8
ROWS = 8
LOW = 2
COLS = 16
WIDTH = 128
PLANE = ROWS * COLS
SHARE = 864
FAR_FIRST = (4, 3, 5, 2, 6, 1, 7)
TILE = 16
CHUNKS = (pl.ds(0, 64), pl.ds(64, 48))


def shifted(value, step):
    rows = value.shape[0]
    column = lax.rem(lax.broadcasted_iota(jnp.int32, value.shape, 0), COLS)
    edge = 0 if step == 1 else COLS - 1
    return jnp.where(column == edge, 0.0, pltpu.roll(value, step % rows, 0))


def joined(wide):
    left, middle, right = wide[:, :WIDTH], wide[:, WIDTH : 2 * WIDTH], wide[:, 2 * WIDTH :]
    return middle + shifted(left, 1) + shifted(right, -1)


def windows(ref, frames, start, height):
    return jnp.concatenate(
        [
            ref[kt : kt + frames, pl.ds(start + kh, height)].reshape(-1, WIDTH)
            for kt in range(3)
            for kh in range(3)
        ],
        axis=1,
    )


def forward_weight(ref):
    return jnp.concatenate(
        [
            jnp.concatenate(
                [ref[(3 * k + kw) * WIDTH : (3 * k + kw + 1) * WIDTH] for k in range(9)], axis=0
            )
            for kw in range(3)
        ],
        axis=1,
    )


def backward_weight(ref):
    return jnp.concatenate(
        [
            jnp.concatenate(
                [
                    ref[(26 - 3 * k - kw) * WIDTH : (27 - 3 * k - kw) * WIDTH]
                    for k in range(9)
                ],
                axis=1,
            )
            for kw in range(3)
        ],
        axis=0,
    )


def kernel(
    scale, video_ref, cotangent_ref, weight_one_ref, weight_two_ref, before_in, count_in,
    output_ref, grads_ref,
    before_ref, count_ref, result_out, first, second, own_video, cotangent_in, ext_both, ext_delta, cache, own_delta, next_delta, slope, deltas,
    part, swap_out, swap_in, total, stage, land_a, land_b, wide,
    load, store, v_send, v_recv, vh_send, vh_recv, d_send, d_recv, dh_send, dh_recv, h_send, h_recv,
    swap_send, swap_recv, a_send, a_recv, b_send, b_recv, w_send, w_recv, o_send, o_recv,
):
    tm = lax.axis_index("tm")
    space = lax.axis_index("space")
    groups = 2 * SIDE * SIDE
    core = lax.rem(tm, 2)
    chip = tm // 2
    y, z = chip // SIDE, lax.rem(chip, SIDE)
    a = y * (1 - core) + z * core
    b = z * (1 - core) + y * core
    stride_a, stride_b = 8 - 7 * core, 1 + 7 * core

    def along_a(step):
        at = lax.rem(a + step, SIDE)
        return at, (2 * (at * stride_a + b * stride_b) + core, space)

    def along_b(step):
        at = lax.rem(b + step, SIDE)
        return at, (2 * (a * stride_a + at * stride_b) + core, space)

    def beside(step):
        return (tm, lax.rem(space + step, SPACE))

    def later(step):
        return (lax.rem(tm + 1, groups), lax.rem(space + step, SPACE))

    def earlier(step):
        return (lax.rem(tm + groups - 1, groups), lax.rem(space + step, SPACE))

    sibling = (tm + 1 - 2 * core, space)

    barrier = pltpu.get_barrier_semaphore()
    near = [beside(step) for step in range(1, SPACE)]
    near += [later(step) for step in range(SPACE)] + [earlier(step) for step in range(SPACE)]
    distant = [along_a(step)[1] for step in range(1, SIDE)]
    distant += [along_b(step)[1] for step in range(1, SIDE)]
    for device in near:
        pl.semaphore_signal(barrier, inc=1, device_id=device, device_id_type=MESH)
    loads = [
        pltpu.make_async_copy(weight_one_ref, first, load.at[0]),
        pltpu.make_async_copy(weight_two_ref, second, load.at[1]),
    ]
    video_load = pltpu.make_async_copy(video_ref.at[0], own_video, load.at[2])
    cotangent_load = pltpu.make_async_copy(cotangent_ref.at[0], cotangent_in, load.at[3])
    scalars = [
        pltpu.make_async_copy(count_in, count_ref, load.at[4]),
        pltpu.make_async_copy(before_in, before_ref, load.at[5]),
    ]
    for copy in scalars + [cotangent_load, video_load] + loads:
        copy.start()
    for device in distant:
        pl.semaphore_signal(barrier, inc=1, device_id=device, device_id_type=MESH)

    ext_video, ext_hidden = ext_both.at[0], ext_both.at[1]
    blank = jnp.zeros((COLS, WIDTH), HALF)
    for ref, frames in ((ext_video, 10), (ext_delta, 12), (ext_hidden, 10)):
        for frame in range(frames):
            ref[frame, 0] = blank
            ref[frame, ROWS + 1] = blank
    ext_delta[0:2] = jnp.zeros((2, ROWS + 2, COLS, WIDTH), HALF)
    for copy in scalars:
        copy.wait()
    starting = before_ref[0, 0] < 0
    live = [jnp.where(count_ref[0, 0] > frame, 1.0, 0.0) for frame in range(FRAMES)]
    going = jnp.where(starting, 0.0, 1.0)
    cotangent_load.wait()
    for frame in range(FRAMES):
        masked = (live[frame] * cotangent_in[frame].astype(FULL)).astype(HALF)
        own_delta[frame] = masked
        ext_delta[2 + frame, pl.ds(1 + LOW * space, LOW)] = masked
        if frame < 2:
            next_delta[frame] = (going * masked.astype(FULL)).astype(HALF)
    video_load.wait()
    ext_video[2:, pl.ds(1 + LOW * space, LOW)] = own_video[...]
    pl.semaphore_wait(barrier, len(near) + len(distant))

    def send(source, target, send_sem, recv_sem, device):
        copy = pltpu.make_async_remote_copy(
            src_ref=source, dst_ref=target, send_sem=send_sem, recv_sem=recv_sem,
            device_id=device, device_id_type=MESH,
        )
        copy.start()
        return copy

    place = pl.ds(1 + LOW * space, LOW)
    videos, changes = [], []
    for step in (2, 1, 3, 0):
        videos.append(
            send(
                own_video.at[pl.ds(FRAMES - 2, 2)], ext_video.at[pl.ds(0, 2), place],
                vh_send.at[step], vh_recv.at[step], later(step),
            )
        )
        if step:
            videos.append(
                send(
                    own_video, ext_video.at[pl.ds(2, FRAMES), place],
                    v_send.at[step - 1], v_recv.at[step - 1], beside(step),
                )
            )
    for step in (2, 1, 3, 0):
        changes.append(
            send(
                next_delta, ext_delta.at[pl.ds(2 + FRAMES, 2), place],
                dh_send.at[step], dh_recv.at[step], earlier(step),
            )
        )
        if step:
            changes.append(
                send(
                    own_delta, ext_delta.at[pl.ds(2, FRAMES), place],
                    d_send.at[step - 1], d_recv.at[step - 1], beside(step),
                )
            )
    for copy in loads:
        copy.wait()
    for copy in videos:
        copy.wait_recv()
    for frame in range(2):
        ext_video[frame] = jnp.where(starting, ext_video[2], ext_video[frame])

    act = joined(
        jnp.dot(
            windows(ext_video, FRAMES, 0, ROWS), forward_weight(first),
            preferred_element_type=FULL,
        )
    )
    for frame in range(FRAMES):
        value = act[frame * PLANE : (frame + 1) * PLANE]
        sigma = jax.nn.sigmoid(value)
        hidden = (live[frame] * (value * sigma)).astype(HALF)
        slope[frame * PLANE : (frame + 1) * PLANE] = live[frame] * (
            sigma * (1.0 + value * (1.0 - sigma))
        )
        ext_hidden[2 + frame, 1 : 1 + ROWS] = hidden.reshape(ROWS, COLS, WIDTH)
    passing = send(
        ext_hidden.at[pl.ds(FRAMES, 2), pl.ds(1, ROWS)], cache, h_send, h_recv, later(0)
    )

    for copy in changes:
        copy.wait_recv()
    spread = joined(
        lax.dot_general(
            windows(ext_delta, FRAMES + 2, 0, ROWS), backward_weight(second),
            (((1,), (1,)), ((), ())), preferred_element_type=FULL,
        )
    )

    def put(slot, frame, value):
        at = slice(frame * PLANE, (frame + 1) * PLANE)
        deltas[slot, at, 0:WIDTH] = shifted(value, -1).astype(HALF)
        deltas[slot, at, WIDTH : 2 * WIDTH] = value.astype(HALF)
        deltas[slot, at, 2 * WIDTH :] = shifted(value, 1).astype(HALF)

    for frame in range(FRAMES):
        own = spread[(frame + 2) * PLANE : (frame + 3) * PLANE]
        if frame == 0:
            own = own + jnp.where(starting, spread[0:PLANE] + spread[PLANE : 2 * PLANE], 0.0)
        put(0, frame, own * slope[frame * PLANE : (frame + 1) * PLANE])

    for frame in range(FRAMES):
        put(1, frame, ext_delta[2 + frame, 1 : 1 + ROWS].reshape(PLANE, WIDTH).astype(FULL))
    passing.wait_recv()
    for frame in range(2):
        ext_hidden[frame, 1 : 1 + ROWS] = jnp.where(
            starting, ext_hidden[2, 1 : 1 + ROWS], cache[frame]
        )

    def gradient(slot):
        pieces = []
        for step in range(3):
            pair = 2 * space + step
            piece = ext_both[slot, pl.ds(pair // 3, FRAMES), pl.ds(lax.rem(pair, 3), ROWS)]
            pieces.append(piece.reshape(-1, WIDTH))
        term = lax.dot_general(
            jnp.concatenate(pieces, axis=1), deltas[slot],
            (((0,), (0,)), ((), ())), preferred_element_type=FULL,
        )
        for step in range(3):
            for kw in range(3):
                at = (3 * step + kw) * WIDTH
                part[at : at + WIDTH] = term[
                    step * WIDTH : (step + 1) * WIDTH, kw * WIDTH : (kw + 1) * WIDTH
                ]
        return part[pl.ds(pl.multiple_of(96 * space, 32), SHARE)]

    swap_out[...] = gradient(1 - core).astype(HALF)
    swap = send(swap_out, swap_in, swap_send, swap_recv, sibling)
    total[0:SHARE] = gradient(core)
    total[SHARE:] = jnp.zeros((SIDE * BLOCK - SHARE, WIDTH), FULL)
    swap.wait_recv()
    total[0:SHARE] += swap_in[...].astype(FULL)
    stage[...] = total[...].astype(HALF).reshape(stage.shape)

    def phase(number, chunk, source, target, send_sem, recv_sem, along):
        for step in FAR_FIRST:
            at, device = along(step)
            send(
                source(at), target(step), send_sem.at[number], recv_sem.at[number], device
            )
        seven = land_a.at[pl.ds(0, SIDE - 1), chunk]
        return (
            pltpu.make_async_copy(seven, seven, send_sem.at[number]),
            pltpu.make_async_copy(seven, seven, recv_sem.at[number]),
        )

    over_a = [
        phase(
            number, chunk, lambda at: stage.at[at, chunk], lambda step: land_a.at[step - 1, chunk],
            a_send, a_recv, along_a,
        )
        for number, chunk in enumerate(CHUNKS)
    ]
    for copy in videos + changes + [passing, swap]:
        copy.wait_send()

    result = joined(
        jnp.dot(
            windows(ext_hidden, FRAMES, LOW * space, LOW), forward_weight(second),
            preferred_element_type=FULL,
        )
    ).reshape(FRAMES, LOW * COLS, WIDTH)
    for frame in range(FRAMES):
        value = own_video[frame].reshape(LOW * COLS, WIDTH).astype(FULL) + result[frame]
        result_out[frame] = (live[frame] * value).astype(HALF).reshape(LOW, COLS, WIDTH)
    stores = [pltpu.make_async_copy(result_out, output_ref.at[0], store.at[0])]
    stores[0].start()

    over_b = []
    for number, chunk in enumerate(CHUNKS):
        block = total[pl.ds(pl.multiple_of(a * BLOCK + chunk.start, TILE), chunk.size)]
        over_a[number][1].wait()
        for step in range(1, SIDE):
            block = block + land_a[step - 1, chunk].astype(FULL)
        land_b[b, chunk] = block.astype(HALF)
        over_b.append(
            phase(
                number, chunk, lambda at: land_b.at[b, chunk], lambda step: land_b.at[b, chunk],
                b_send, b_recv, along_b,
            )
        )
    for copy, _ in over_a:
        copy.wait()
    back = []
    for number, chunk in enumerate(CHUNKS):
        over_b[number][1].wait()
        block = land_b[0, chunk].astype(FULL)
        for at in range(1, SIDE):
            block = block + land_b[at, chunk].astype(FULL)
        wide[a, chunk] = (block * scale).astype(HALF)
        for step in FAR_FIRST:
            back.append(
                send(
                    wide.at[a, chunk], wide.at[a, chunk],
                    w_send.at[number, step - 1], w_recv.at[number, step - 1], along_a(step)[1],
                )
            )
    for copy, _ in over_b:
        copy.wait()
    across = []
    for number, chunk in enumerate(CHUNKS):
        for copy in back[(SIDE - 1) * number : (SIDE - 1) * (number + 1)]:
            copy.wait_recv()
        across.append(
            send(
                wide.at[:, chunk], grads_ref.at[core, :, chunk],
                o_send.at[number], o_recv.at[number], sibling,
            )
        )
    stores.append(pltpu.make_async_copy(wide, grads_ref.at[core], store.at[1]))
    stores[1].start()
    for copy in back:
        copy.wait_send()
    for copy in across:
        copy.wait()
    for copy in stores:
        copy.wait()


def per_device(video, cotangent, weight_one, weight_two, predecessor, frame_count):
    frames, height, columns, width = video.shape[1:]
    groups, parts = lax.axis_size("tm"), lax.axis_size("space")
    scale = 1.0 / math.sqrt(groups * parts * frames * height * columns)
    far = pl.BlockSpec(memory_space=pltpu.HBM)
    dma = pltpu.SemaphoreType.DMA
    taps = weight_one.shape[0]
    blocks = (SIDE, BLOCK, WIDTH)
    output, grads = pl.pallas_call(
        lambda *refs: kernel(scale, *refs),
        out_shape=(
            jax.ShapeDtypeStruct(video.shape, HALF),
            jax.ShapeDtypeStruct((2,) + blocks, HALF),
        ),
        in_specs=[far] * 6,
        out_specs=(far, far),
        scratch_shapes=[
            pltpu.SMEM((1, 1), jnp.int32),
            pltpu.SMEM((1, 1), jnp.int32),
            pltpu.VMEM((FRAMES, LOW, COLS, WIDTH), HALF),
            pltpu.VMEM((taps, WIDTH), HALF),
            pltpu.VMEM((taps, WIDTH), HALF),
            pltpu.VMEM((FRAMES, LOW, COLS, WIDTH), HALF),
            pltpu.VMEM((FRAMES, LOW, COLS, WIDTH), HALF),
            pltpu.VMEM((2, FRAMES + 2, ROWS + 2, COLS, WIDTH), HALF),
            pltpu.VMEM((FRAMES + 4, ROWS + 2, COLS, WIDTH), HALF),
            pltpu.VMEM((2, ROWS, COLS, WIDTH), HALF),
            pltpu.VMEM((FRAMES, LOW, COLS, WIDTH), HALF),
            pltpu.VMEM((2, LOW, COLS, WIDTH), HALF),
            pltpu.VMEM((FRAMES * PLANE, WIDTH), FULL),
            pltpu.VMEM((2, FRAMES * PLANE, 3 * WIDTH), HALF),
            pltpu.VMEM((9 * WIDTH, WIDTH), FULL),
            pltpu.VMEM((SHARE, WIDTH), HALF),
            pltpu.VMEM((SHARE, WIDTH), HALF),
            pltpu.VMEM((SIDE * BLOCK, WIDTH), FULL),
            pltpu.VMEM(blocks, HALF),
            pltpu.VMEM((SIDE - 1, BLOCK, WIDTH), HALF),
            pltpu.VMEM(blocks, HALF),
            pltpu.VMEM(blocks, HALF),
            dma((6,)),
            dma((2,)),
            dma((SPACE - 1,)),
            dma((SPACE - 1,)),
            dma((SPACE,)),
            dma((SPACE,)),
            dma((SPACE - 1,)),
            dma((SPACE - 1,)),
            dma((SPACE,)),
            dma((SPACE,)),
            dma,
            dma,
            dma,
            dma,
            dma((len(CHUNKS),)),
            dma((len(CHUNKS),)),
            dma((len(CHUNKS),)),
            dma((len(CHUNKS),)),
            dma((len(CHUNKS), SIDE - 1)),
            dma((len(CHUNKS), SIDE - 1)),
            dma((2,)),
            dma((2,)),
        ],
        compiler_params=pltpu.CompilerParams(
            collective_id=0, has_side_effects=True, vmem_limit_bytes=62 * 1024 * 1024
        ),
    )(
        video, cotangent, weight_one, weight_two,
        predecessor.reshape(1, 1), frame_count.reshape(1, 1),
    )

    flat = grads.reshape(-1, WIDTH)

    def widened(number):
        begin = number * SIDE * BLOCK
        return flat[begin : begin + taps // parts].astype(FULL)

    return (output, widened(0), widened(1))


def solution(mesh):
    placed = (
        P("tm", None, "space", None, None),
        P("tm", None, "space", None, None),
        P(),
        P(),
        P("tm"),
        P("tm"),
    )
    return jax.shard_map(
        per_device,
        mesh=mesh,
        in_specs=placed,
        out_specs=(P("tm", None, "space", None, None), P("space", None), P("space", None)),
        check_vma=False,
    )
```

```python
import math

import jax
import jax.numpy as jnp
from jax import lax
from jax.experimental import pallas as pl
from jax.experimental.pallas import tpu as pltpu
from jax.sharding import PartitionSpec as P

MESH = pl.DeviceIdType.MESH
HALF = jnp.bfloat16
FULL = jnp.float32
SIDE = 8
SPACE = 4
BLOCK = 112
FRAMES = 8
ROWS = 8
LOW = 2
COLS = 16
WIDTH = 128
PLANE = ROWS * COLS
SHARE = 864
FAR_FIRST = (4, 3, 5, 2, 6, 1, 7)
TILE = 16
CHUNKS = (pl.ds(0, 64), pl.ds(64, 48))


def shifted(value, step):
    rows = value.shape[0]
    column = lax.rem(lax.broadcasted_iota(jnp.int32, value.shape, 0), COLS)
    edge = 0 if step == 1 else COLS - 1
    return jnp.where(column == edge, 0.0, pltpu.roll(value, step % rows, 0))


def joined(wide):
    left, middle, right = wide[:, :WIDTH], wide[:, WIDTH : 2 * WIDTH], wide[:, 2 * WIDTH :]
    return middle + shifted(left, 1) + shifted(right, -1)


def windows(ref, begin, frames, start, height):
    return jnp.concatenate(
        [
            ref[begin + kt : begin + kt + frames, pl.ds(start + kh, height)].reshape(-1, WIDTH)
            for kt in range(3)
            for kh in range(3)
        ],
        axis=1,
    )


def forward_weight(ref):
    return jnp.concatenate(
        [
            jnp.concatenate(
                [ref[(3 * k + kw) * WIDTH : (3 * k + kw + 1) * WIDTH] for k in range(9)], axis=0
            )
            for kw in range(3)
        ],
        axis=1,
    )


def backward_weight(ref):
    return jnp.concatenate(
        [
            jnp.concatenate(
                [
                    ref[(26 - 3 * k - kw) * WIDTH : (27 - 3 * k - kw) * WIDTH]
                    for k in range(9)
                ],
                axis=1,
            )
            for kw in range(3)
        ],
        axis=0,
    )


def kernel(
    scale, video_ref, cotangent_ref, weight_one_ref, weight_two_ref, before_in, count_in,
    output_ref, grads_ref,
    before_ref, count_ref, result_out, first, second, own_video, cotangent_in, ext_both, ext_delta, cache, own_delta, next_delta, slope, deltas,
    part, swap_out, swap_in, total, stage, land_a, land_b, wide,
    load, store, v_send, v_recv, vh_send, vh_recv, d_send, d_recv, dh_send, dh_recv, h_send, h_recv,
    swap_send, swap_recv, a_send, a_recv, b_send, b_recv, w_send, w_recv, o_send, o_recv,
):
    tm = lax.axis_index("tm")
    space = lax.axis_index("space")
    groups = 2 * SIDE * SIDE
    core = lax.rem(tm, 2)
    chip = tm // 2
    y, z = chip // SIDE, lax.rem(chip, SIDE)
    a = y * (1 - core) + z * core
    b = z * (1 - core) + y * core
    stride_a, stride_b = 8 - 7 * core, 1 + 7 * core

    def along_a(step):
        at = lax.rem(a + step, SIDE)
        return at, (2 * (at * stride_a + b * stride_b) + core, space)

    def along_b(step):
        at = lax.rem(b + step, SIDE)
        return at, (2 * (a * stride_a + at * stride_b) + core, space)

    def beside(step):
        return (tm, lax.rem(space + step, SPACE))

    def later(step):
        return (lax.rem(tm + 1, groups), lax.rem(space + step, SPACE))

    def earlier(step):
        return (lax.rem(tm + groups - 1, groups), lax.rem(space + step, SPACE))

    sibling = (tm + 1 - 2 * core, space)

    barrier = pltpu.get_barrier_semaphore()
    near = [beside(step) for step in range(1, SPACE)]
    near += [later(step) for step in range(SPACE)] + [earlier(step) for step in range(SPACE)]
    distant = [along_a(step)[1] for step in range(1, SIDE)]
    distant += [along_b(step)[1] for step in range(1, SIDE)]
    for device in near:
        pl.semaphore_signal(barrier, inc=1, device_id=device, device_id_type=MESH)
    loads = [
        pltpu.make_async_copy(weight_one_ref, first, load.at[0]),
        pltpu.make_async_copy(weight_two_ref, second, load.at[1]),
    ]
    video_load = pltpu.make_async_copy(video_ref.at[0], own_video, load.at[2])
    cotangent_load = pltpu.make_async_copy(cotangent_ref.at[0], cotangent_in, load.at[3])
    scalars = [
        pltpu.make_async_copy(count_in, count_ref, load.at[4]),
        pltpu.make_async_copy(before_in, before_ref, load.at[5]),
    ]
    for copy in scalars + [cotangent_load, video_load] + loads:
        copy.start()
    for device in distant:
        pl.semaphore_signal(barrier, inc=1, device_id=device, device_id_type=MESH)

    ext_video, ext_hidden = ext_both.at[0], ext_both.at[1]
    blank = jnp.zeros((COLS, WIDTH), HALF)
    for ref, frames in ((ext_video, 10), (ext_delta, 12), (ext_hidden, 10)):
        for frame in range(frames):
            ref[frame, 0] = blank
            ref[frame, ROWS + 1] = blank
    ext_delta[0:2] = jnp.zeros((2, ROWS + 2, COLS, WIDTH), HALF)
    for copy in scalars:
        copy.wait()
    starting = before_ref[0, 0] < 0
    live = [jnp.where(count_ref[0, 0] > frame, 1.0, 0.0) for frame in range(FRAMES)]
    going = jnp.where(starting, 0.0, 1.0)
    cotangent_load.wait()
    for frame in range(FRAMES):
        masked = (live[frame] * cotangent_in[frame].astype(FULL)).astype(HALF)
        own_delta[frame] = masked
        ext_delta[2 + frame, pl.ds(1 + LOW * space, LOW)] = masked
        if frame < 2:
            next_delta[frame] = (going * masked.astype(FULL)).astype(HALF)
    video_load.wait()
    ext_video[2:, pl.ds(1 + LOW * space, LOW)] = own_video[...]
    pl.semaphore_wait(barrier, len(near) + len(distant))

    def send(source, target, send_sem, recv_sem, device):
        copy = pltpu.make_async_remote_copy(
            src_ref=source, dst_ref=target, send_sem=send_sem, recv_sem=recv_sem,
            device_id=device, device_id_type=MESH,
        )
        copy.start()
        return copy

    place = pl.ds(1 + LOW * space, LOW)
    videos, changes = [], []
    for step in (2, 1, 3, 0):
        videos.append(
            send(
                own_video.at[pl.ds(FRAMES - 2, 2)], ext_video.at[pl.ds(0, 2), place],
                vh_send.at[step], vh_recv.at[step], later(step),
            )
        )
        if step:
            videos.append(
                send(
                    own_video, ext_video.at[pl.ds(2, FRAMES), place],
                    v_send.at[step - 1], v_recv.at[step - 1], beside(step),
                )
            )
    for step in (2, 1, 3):
        changes.append(
            send(
                own_delta, ext_delta.at[pl.ds(2, FRAMES), place],
                d_send.at[step - 1], d_recv.at[step - 1], beside(step),
            )
        )
    following = [
        send(
            next_delta, ext_delta.at[pl.ds(2 + FRAMES, 2), place],
            dh_send.at[step], dh_recv.at[step], earlier(step),
        )
        for step in (2, 1, 3, 0)
    ]
    for copy in loads:
        copy.wait()
    for copy in videos:
        copy.wait_recv()
    for frame in range(2):
        ext_video[frame] = jnp.where(starting, ext_video[2], ext_video[frame])

    weight = forward_weight(first)
    count = FRAMES // 2
    for begin in range(0, FRAMES, count):
        act = joined(
            jnp.dot(
                windows(ext_video, begin, count, 0, ROWS), weight, preferred_element_type=FULL
            )
        )
        for frame in range(begin, begin + count):
            value = act[(frame - begin) * PLANE : (frame - begin + 1) * PLANE]
            sigma = jax.nn.sigmoid(value)
            hidden = (live[frame] * (value * sigma)).astype(HALF)
            slope[frame * PLANE : (frame + 1) * PLANE] = live[frame] * (
                sigma * (1.0 + value * (1.0 - sigma))
            )
            ext_hidden[2 + frame, 1 : 1 + ROWS] = hidden.reshape(ROWS, COLS, WIDTH)
    passing = send(
        ext_hidden.at[pl.ds(FRAMES, 2), pl.ds(1, ROWS)], cache, h_send, h_recv, later(0)
    )

    for copy in changes:
        copy.wait_recv()
    def put(slot, frame, value):
        at = slice(frame * PLANE, (frame + 1) * PLANE)
        deltas[slot, at, 0:WIDTH] = shifted(value, -1).astype(HALF)
        deltas[slot, at, WIDTH : 2 * WIDTH] = value.astype(HALF)
        deltas[slot, at, 2 * WIDTH :] = shifted(value, 1).astype(HALF)

    for frame in range(FRAMES):
        put(1, frame, ext_delta[2 + frame, 1 : 1 + ROWS].reshape(PLANE, WIDTH).astype(FULL))
    weight = backward_weight(second)
    count = (FRAMES + 2) // 2
    early = 0.0
    for begin in range(0, FRAMES + 2, count):
        if begin:
            for copy in following:
                copy.wait_recv()
        spread = joined(
            lax.dot_general(
                windows(ext_delta, begin, count, 0, ROWS), weight,
                (((1,), (1,)), ((), ())), preferred_element_type=FULL,
            )
        )
        for frame in range(begin, begin + count):
            own = spread[(frame - begin) * PLANE : (frame - begin + 1) * PLANE]
            if frame < 2:
                early = early + own
                continue
            if frame == 2:
                own = own + jnp.where(starting, early, 0.0)
            put(0, frame - 2, own * slope[(frame - 2) * PLANE : (frame - 1) * PLANE])
    passing.wait_recv()
    for frame in range(2):
        ext_hidden[frame, 1 : 1 + ROWS] = jnp.where(
            starting, ext_hidden[2, 1 : 1 + ROWS], cache[frame]
        )

    def gradient(slot):
        pieces = []
        for step in range(3):
            pair = 2 * space + step
            piece = ext_both[slot, pl.ds(pair // 3, FRAMES), pl.ds(lax.rem(pair, 3), ROWS)]
            pieces.append(piece.reshape(-1, WIDTH))
        term = lax.dot_general(
            jnp.concatenate(pieces, axis=1), deltas[slot],
            (((0,), (0,)), ((), ())), preferred_element_type=FULL,
        )
        for step in range(3):
            for kw in range(3):
                at = (3 * step + kw) * WIDTH
                part[at : at + WIDTH] = term[
                    step * WIDTH : (step + 1) * WIDTH, kw * WIDTH : (kw + 1) * WIDTH
                ]
        return part[pl.ds(pl.multiple_of(96 * space, 32), SHARE)]

    swap_out[...] = gradient(1 - core).astype(HALF)
    swap = send(swap_out, swap_in, swap_send, swap_recv, sibling)
    total[0:SHARE] = gradient(core)
    total[SHARE:] = jnp.zeros((SIDE * BLOCK - SHARE, WIDTH), FULL)
    swap.wait_recv()
    total[0:SHARE] += swap_in[...].astype(FULL)
    stage[...] = total[...].astype(HALF).reshape(stage.shape)

    def phase(number, chunk, source, target, send_sem, recv_sem, along):
        for step in FAR_FIRST:
            at, device = along(step)
            send(
                source(at), target(step), send_sem.at[number], recv_sem.at[number], device
            )
        seven = land_a.at[pl.ds(0, SIDE - 1), chunk]
        return (
            pltpu.make_async_copy(seven, seven, send_sem.at[number]),
            pltpu.make_async_copy(seven, seven, recv_sem.at[number]),
        )

    over_a = [
        phase(
            number, chunk, lambda at: stage.at[at, chunk], lambda step: land_a.at[step - 1, chunk],
            a_send, a_recv, along_a,
        )
        for number, chunk in enumerate(CHUNKS)
    ]
    for copy in videos + changes + following + [passing, swap]:
        copy.wait_send()

    result = joined(
        jnp.dot(
            windows(ext_hidden, 0, FRAMES, LOW * space, LOW), forward_weight(second),
            preferred_element_type=FULL,
        )
    ).reshape(FRAMES, LOW * COLS, WIDTH)
    for frame in range(FRAMES):
        value = own_video[frame].reshape(LOW * COLS, WIDTH).astype(FULL) + result[frame]
        result_out[frame] = (live[frame] * value).astype(HALF).reshape(LOW, COLS, WIDTH)
    stores = [pltpu.make_async_copy(result_out, output_ref.at[0], store.at[0])]
    stores[0].start()

    over_b = []
    for number, chunk in enumerate(CHUNKS):
        block = total[pl.ds(pl.multiple_of(a * BLOCK + chunk.start, TILE), chunk.size)]
        over_a[number][1].wait()
        for step in range(1, SIDE):
            block = block + land_a[step - 1, chunk].astype(FULL)
        land_b[b, chunk] = block.astype(HALF)
        over_b.append(
            phase(
                number, chunk, lambda at: land_b.at[b, chunk], lambda step: land_b.at[b, chunk],
                b_send, b_recv, along_b,
            )
        )
    for copy, _ in over_a:
        copy.wait()
    back = []
    for number, chunk in enumerate(CHUNKS):
        over_b[number][1].wait()
        block = land_b[0, chunk].astype(FULL)
        for at in range(1, SIDE):
            block = block + land_b[at, chunk].astype(FULL)
        wide[a, chunk] = (block * scale).astype(HALF)
        for step in FAR_FIRST:
            back.append(
                send(
                    wide.at[a, chunk], wide.at[a, chunk],
                    w_send.at[number, step - 1], w_recv.at[number, step - 1], along_a(step)[1],
                )
            )
    for copy, _ in over_b:
        copy.wait()
    across = []
    for number, chunk in enumerate(CHUNKS):
        for copy in back[(SIDE - 1) * number : (SIDE - 1) * (number + 1)]:
            copy.wait_recv()
        across.append(
            send(
                wide.at[:, chunk], grads_ref.at[core, :, chunk],
                o_send.at[number], o_recv.at[number], sibling,
            )
        )
    stores.append(pltpu.make_async_copy(wide, grads_ref.at[core], store.at[1]))
    stores[1].start()
    for copy in back:
        copy.wait_send()
    for copy in across:
        copy.wait()
    for copy in stores:
        copy.wait()


def per_device(video, cotangent, weight_one, weight_two, predecessor, frame_count):
    frames, height, columns, width = video.shape[1:]
    groups, parts = lax.axis_size("tm"), lax.axis_size("space")
    scale = 1.0 / math.sqrt(groups * parts * frames * height * columns)
    far = pl.BlockSpec(memory_space=pltpu.HBM)
    dma = pltpu.SemaphoreType.DMA
    taps = weight_one.shape[0]
    blocks = (SIDE, BLOCK, WIDTH)
    output, grads = pl.pallas_call(
        lambda *refs: kernel(scale, *refs),
        out_shape=(
            jax.ShapeDtypeStruct(video.shape, HALF),
            jax.ShapeDtypeStruct((2,) + blocks, HALF),
        ),
        in_specs=[far] * 6,
        out_specs=(far, far),
        scratch_shapes=[
            pltpu.SMEM((1, 1), jnp.int32),
            pltpu.SMEM((1, 1), jnp.int32),
            pltpu.VMEM((FRAMES, LOW, COLS, WIDTH), HALF),
            pltpu.VMEM((taps, WIDTH), HALF),
            pltpu.VMEM((taps, WIDTH), HALF),
            pltpu.VMEM((FRAMES, LOW, COLS, WIDTH), HALF),
            pltpu.VMEM((FRAMES, LOW, COLS, WIDTH), HALF),
            pltpu.VMEM((2, FRAMES + 2, ROWS + 2, COLS, WIDTH), HALF),
            pltpu.VMEM((FRAMES + 4, ROWS + 2, COLS, WIDTH), HALF),
            pltpu.VMEM((2, ROWS, COLS, WIDTH), HALF),
            pltpu.VMEM((FRAMES, LOW, COLS, WIDTH), HALF),
            pltpu.VMEM((2, LOW, COLS, WIDTH), HALF),
            pltpu.VMEM((FRAMES * PLANE, WIDTH), FULL),
            pltpu.VMEM((2, FRAMES * PLANE, 3 * WIDTH), HALF),
            pltpu.VMEM((9 * WIDTH, WIDTH), FULL),
            pltpu.VMEM((SHARE, WIDTH), HALF),
            pltpu.VMEM((SHARE, WIDTH), HALF),
            pltpu.VMEM((SIDE * BLOCK, WIDTH), FULL),
            pltpu.VMEM(blocks, HALF),
            pltpu.VMEM((SIDE - 1, BLOCK, WIDTH), HALF),
            pltpu.VMEM(blocks, HALF),
            pltpu.VMEM(blocks, HALF),
            dma((6,)),
            dma((2,)),
            dma((SPACE - 1,)),
            dma((SPACE - 1,)),
            dma((SPACE,)),
            dma((SPACE,)),
            dma((SPACE - 1,)),
            dma((SPACE - 1,)),
            dma((SPACE,)),
            dma((SPACE,)),
            dma,
            dma,
            dma,
            dma,
            dma((len(CHUNKS),)),
            dma((len(CHUNKS),)),
            dma((len(CHUNKS),)),
            dma((len(CHUNKS),)),
            dma((len(CHUNKS), SIDE - 1)),
            dma((len(CHUNKS), SIDE - 1)),
            dma((2,)),
            dma((2,)),
        ],
        compiler_params=pltpu.CompilerParams(
            collective_id=0, has_side_effects=True, vmem_limit_bytes=62 * 1024 * 1024
        ),
    )(
        video, cotangent, weight_one, weight_two,
        predecessor.reshape(1, 1), frame_count.reshape(1, 1),
    )

    flat = grads.reshape(-1, WIDTH)

    def widened(number):
        begin = number * SIDE * BLOCK
        return flat[begin : begin + taps // parts].astype(FULL)

    return (output, widened(0), widened(1))


def solution(mesh):
    placed = (
        P("tm", None, "space", None, None),
        P("tm", None, "space", None, None),
        P(),
        P(),
        P("tm"),
        P("tm"),
    )
    return jax.shard_map(
        per_device,
        mesh=mesh,
        in_specs=placed,
        out_specs=(P("tm", None, "space", None, None), P("space", None), P("space", None)),
        check_vma=False,
    )
```

```python
import math

import jax
import jax.numpy as jnp
from jax import lax
from jax.experimental import pallas as pl
from jax.experimental.pallas import tpu as pltpu
from jax.sharding import PartitionSpec as P

MESH = pl.DeviceIdType.MESH
HALF = jnp.bfloat16
FULL = jnp.float32
SIDE = 8
SPACE = 4
BLOCK = 112
FRAMES = 8
ROWS = 8
LOW = 2
COLS = 16
WIDTH = 128
PLANE = ROWS * COLS
SHARE = 864
FAR_FIRST = (4, 3, 5, 2, 6, 1, 7)
TILE = 16
CHUNKS = (pl.ds(0, 48), pl.ds(48, 64))


def shifted(value, step):
    rows = value.shape[0]
    column = lax.rem(lax.broadcasted_iota(jnp.int32, value.shape, 0), COLS)
    edge = 0 if step == 1 else COLS - 1
    return jnp.where(column == edge, 0.0, pltpu.roll(value, step % rows, 0))


def joined(wide):
    left, middle, right = wide[:, :WIDTH], wide[:, WIDTH : 2 * WIDTH], wide[:, 2 * WIDTH :]
    return middle + shifted(left, 1) + shifted(right, -1)


def windows(ref, begin, frames, start, height):
    return jnp.concatenate(
        [
            ref[begin + kt : begin + kt + frames, pl.ds(start + kh, height)].reshape(-1, WIDTH)
            for kt in range(3)
            for kh in range(3)
        ],
        axis=1,
    )


def forward_weight(ref):
    return jnp.concatenate(
        [
            jnp.concatenate(
                [ref[(3 * k + kw) * WIDTH : (3 * k + kw + 1) * WIDTH] for k in range(9)], axis=0
            )
            for kw in range(3)
        ],
        axis=1,
    )


def backward_weight(ref):
    return jnp.concatenate(
        [
            jnp.concatenate(
                [
                    ref[(26 - 3 * k - kw) * WIDTH : (27 - 3 * k - kw) * WIDTH]
                    for k in range(9)
                ],
                axis=1,
            )
            for kw in range(3)
        ],
        axis=0,
    )


def kernel(
    scale, video_ref, cotangent_ref, weight_one_ref, weight_two_ref, before_in, count_in,
    output_ref, grads_ref,
    before_ref, count_ref, result_out, first, second, own_video, cotangent_in, ext_both, ext_delta, cache, own_delta, next_delta, slope, deltas,
    part, swap_out, swap_in, total, stage, land_a, land_b, wide,
    load, store, v_send, v_recv, vh_send, vh_recv, d_send, d_recv, dh_send, dh_recv, h_send, h_recv,
    swap_send, swap_recv, a_send, a_recv, b_send, b_recv, w_send, w_recv, o_send, o_recv,
):
    tm = lax.axis_index("tm")
    space = lax.axis_index("space")
    groups = 2 * SIDE * SIDE
    core = lax.rem(tm, 2)
    chip = tm // 2
    y, z = chip // SIDE, lax.rem(chip, SIDE)
    a = y * (1 - core) + z * core
    b = z * (1 - core) + y * core
    stride_a, stride_b = 8 - 7 * core, 1 + 7 * core

    def along_a(step):
        at = lax.rem(a + step, SIDE)
        return at, (2 * (at * stride_a + b * stride_b) + core, space)

    def along_b(step):
        at = lax.rem(b + step, SIDE)
        return at, (2 * (a * stride_a + at * stride_b) + core, space)

    def beside(step):
        return (tm, lax.rem(space + step, SPACE))

    def later(step):
        return (lax.rem(tm + 1, groups), lax.rem(space + step, SPACE))

    def earlier(step):
        return (lax.rem(tm + groups - 1, groups), lax.rem(space + step, SPACE))

    sibling = (tm + 1 - 2 * core, space)

    barrier = pltpu.get_barrier_semaphore()
    near = [beside(step) for step in range(1, SPACE)]
    near += [later(step) for step in range(SPACE)] + [earlier(step) for step in range(SPACE)]
    distant = [along_a(step)[1] for step in range(1, SIDE)]
    distant += [along_b(step)[1] for step in range(1, SIDE)]
    for device in near:
        pl.semaphore_signal(barrier, inc=1, device_id=device, device_id_type=MESH)
    loads = [
        pltpu.make_async_copy(weight_one_ref, first, load.at[0]),
        pltpu.make_async_copy(weight_two_ref, second, load.at[1]),
    ]
    video_load = pltpu.make_async_copy(video_ref.at[0], own_video, load.at[2])
    cotangent_load = pltpu.make_async_copy(cotangent_ref.at[0], cotangent_in, load.at[3])
    scalars = [
        pltpu.make_async_copy(count_in, count_ref, load.at[4]),
        pltpu.make_async_copy(before_in, before_ref, load.at[5]),
    ]
    for copy in scalars + [cotangent_load, video_load] + loads:
        copy.start()
    for device in distant:
        pl.semaphore_signal(barrier, inc=1, device_id=device, device_id_type=MESH)

    ext_video, ext_hidden = ext_both.at[0], ext_both.at[1]
    blank = jnp.zeros((COLS, WIDTH), HALF)
    for ref, frames in ((ext_video, 10), (ext_delta, 12), (ext_hidden, 10)):
        for frame in range(frames):
            ref[frame, 0] = blank
            ref[frame, ROWS + 1] = blank
    ext_delta[0:2] = jnp.zeros((2, ROWS + 2, COLS, WIDTH), HALF)
    for copy in scalars:
        copy.wait()
    starting = before_ref[0, 0] < 0
    live = [jnp.where(count_ref[0, 0] > frame, 1.0, 0.0) for frame in range(FRAMES)]
    going = jnp.where(starting, 0.0, 1.0)
    cotangent_load.wait()
    for frame in range(FRAMES):
        masked = (live[frame] * cotangent_in[frame].astype(FULL)).astype(HALF)
        own_delta[frame] = masked
        ext_delta[2 + frame, pl.ds(1 + LOW * space, LOW)] = masked
        if frame < 2:
            next_delta[frame] = (going * masked.astype(FULL)).astype(HALF)
    video_load.wait()
    ext_video[2:, pl.ds(1 + LOW * space, LOW)] = own_video[...]
    pl.semaphore_wait(barrier, len(near) + len(distant))

    def send(source, target, send_sem, recv_sem, device):
        copy = pltpu.make_async_remote_copy(
            src_ref=source, dst_ref=target, send_sem=send_sem, recv_sem=recv_sem,
            device_id=device, device_id_type=MESH,
        )
        copy.start()
        return copy

    place = pl.ds(1 + LOW * space, LOW)
    videos, changes = [], []
    for step in (2, 1, 3, 0):
        videos.append(
            send(
                own_video.at[pl.ds(FRAMES - 2, 2)], ext_video.at[pl.ds(0, 2), place],
                vh_send.at[step], vh_recv.at[step], later(step),
            )
        )
        if step:
            videos.append(
                send(
                    own_video, ext_video.at[pl.ds(2, FRAMES), place],
                    v_send.at[step - 1], v_recv.at[step - 1], beside(step),
                )
            )
    for step in (2, 1, 3):
        changes.append(
            send(
                own_delta, ext_delta.at[pl.ds(2, FRAMES), place],
                d_send.at[step - 1], d_recv.at[step - 1], beside(step),
            )
        )
    following = [
        send(
            next_delta, ext_delta.at[pl.ds(2 + FRAMES, 2), place],
            dh_send.at[step], dh_recv.at[step], earlier(step),
        )
        for step in (2, 1, 3, 0)
    ]
    for copy in loads:
        copy.wait()
    for copy in videos:
        copy.wait_recv()
    for frame in range(2):
        ext_video[frame] = jnp.where(starting, ext_video[2], ext_video[frame])

    weight = forward_weight(first)
    count = FRAMES // 2
    for begin in range(0, FRAMES, count):
        act = joined(
            jnp.dot(
                windows(ext_video, begin, count, 0, ROWS), weight, preferred_element_type=FULL
            )
        )
        for frame in range(begin, begin + count):
            value = act[(frame - begin) * PLANE : (frame - begin + 1) * PLANE]
            sigma = jax.nn.sigmoid(value)
            hidden = (live[frame] * (value * sigma)).astype(HALF)
            slope[frame * PLANE : (frame + 1) * PLANE] = live[frame] * (
                sigma * (1.0 + value * (1.0 - sigma))
            )
            ext_hidden[2 + frame, 1 : 1 + ROWS] = hidden.reshape(ROWS, COLS, WIDTH)
    passing = send(
        ext_hidden.at[pl.ds(FRAMES, 2), pl.ds(1, ROWS)], cache, h_send, h_recv, later(0)
    )

    for copy in changes:
        copy.wait_recv()
    def put(slot, frame, value):
        at = slice(frame * PLANE, (frame + 1) * PLANE)
        deltas[slot, at, 0:WIDTH] = shifted(value, -1).astype(HALF)
        deltas[slot, at, WIDTH : 2 * WIDTH] = value.astype(HALF)
        deltas[slot, at, 2 * WIDTH :] = shifted(value, 1).astype(HALF)

    for frame in range(FRAMES):
        put(1, frame, ext_delta[2 + frame, 1 : 1 + ROWS].reshape(PLANE, WIDTH).astype(FULL))
    weight = backward_weight(second)
    count = (FRAMES + 2) // 2
    early = 0.0
    for begin in range(0, FRAMES + 2, count):
        if begin:
            for copy in following:
                copy.wait_recv()
        spread = joined(
            lax.dot_general(
                windows(ext_delta, begin, count, 0, ROWS), weight,
                (((1,), (1,)), ((), ())), preferred_element_type=FULL,
            )
        )
        for frame in range(begin, begin + count):
            own = spread[(frame - begin) * PLANE : (frame - begin + 1) * PLANE]
            if frame < 2:
                early = early + own
                continue
            if frame == 2:
                own = own + jnp.where(starting, early, 0.0)
            put(0, frame - 2, own * slope[(frame - 2) * PLANE : (frame - 1) * PLANE])
    passing.wait_recv()
    for frame in range(2):
        ext_hidden[frame, 1 : 1 + ROWS] = jnp.where(
            starting, ext_hidden[2, 1 : 1 + ROWS], cache[frame]
        )

    def gradient(slot):
        pieces = []
        for step in range(3):
            pair = 2 * space + step
            piece = ext_both[slot, pl.ds(pair // 3, FRAMES), pl.ds(lax.rem(pair, 3), ROWS)]
            pieces.append(piece.reshape(-1, WIDTH))
        term = lax.dot_general(
            jnp.concatenate(pieces, axis=1), deltas[slot],
            (((0,), (0,)), ((), ())), preferred_element_type=FULL,
        )
        for step in range(3):
            for kw in range(3):
                at = (3 * step + kw) * WIDTH
                part[at : at + WIDTH] = term[
                    step * WIDTH : (step + 1) * WIDTH, kw * WIDTH : (kw + 1) * WIDTH
                ]
        return part[pl.ds(pl.multiple_of(96 * space, 32), SHARE)]

    swap_out[...] = gradient(1 - core).astype(HALF)
    swap = send(swap_out, swap_in, swap_send, swap_recv, sibling)
    total[0:SHARE] = gradient(core)
    total[SHARE:] = jnp.zeros((SIDE * BLOCK - SHARE, WIDTH), FULL)
    swap.wait_recv()
    total[0:SHARE] += swap_in[...].astype(FULL)
    stage[...] = total[...].astype(HALF).reshape(stage.shape)

    def phase(number, chunk, source, target, send_sem, recv_sem, along):
        for step in FAR_FIRST:
            at, device = along(step)
            send(
                source(at), target(step), send_sem.at[number], recv_sem.at[number], device
            )
        seven = land_a.at[pl.ds(0, SIDE - 1), chunk]
        return (
            pltpu.make_async_copy(seven, seven, send_sem.at[number]),
            pltpu.make_async_copy(seven, seven, recv_sem.at[number]),
        )

    over_a = [
        phase(
            number, chunk, lambda at: stage.at[at, chunk], lambda step: land_a.at[step - 1, chunk],
            a_send, a_recv, along_a,
        )
        for number, chunk in enumerate(CHUNKS)
    ]
    for copy in videos + changes + following + [passing, swap]:
        copy.wait_send()

    result = joined(
        jnp.dot(
            windows(ext_hidden, 0, FRAMES, LOW * space, LOW), forward_weight(second),
            preferred_element_type=FULL,
        )
    ).reshape(FRAMES, LOW * COLS, WIDTH)
    for frame in range(FRAMES):
        value = own_video[frame].reshape(LOW * COLS, WIDTH).astype(FULL) + result[frame]
        result_out[frame] = (live[frame] * value).astype(HALF).reshape(LOW, COLS, WIDTH)
    stores = [pltpu.make_async_copy(result_out, output_ref.at[0], store.at[0])]
    stores[0].start()

    over_b = []
    for number, chunk in enumerate(CHUNKS):
        block = total[pl.ds(pl.multiple_of(a * BLOCK + chunk.start, TILE), chunk.size)]
        over_a[number][1].wait()
        for step in range(1, SIDE):
            block = block + land_a[step - 1, chunk].astype(FULL)
        land_b[b, chunk] = block.astype(HALF)
        over_b.append(
            phase(
                number, chunk, lambda at: land_b.at[b, chunk], lambda step: land_b.at[b, chunk],
                b_send, b_recv, along_b,
            )
        )
    for copy, _ in over_a:
        copy.wait()
    back = []
    for number, chunk in enumerate(CHUNKS):
        over_b[number][1].wait()
        block = land_b[0, chunk].astype(FULL)
        for at in range(1, SIDE):
            block = block + land_b[at, chunk].astype(FULL)
        wide[a, chunk] = (block * scale).astype(HALF)
        for step in FAR_FIRST:
            back.append(
                send(
                    wide.at[a, chunk], wide.at[a, chunk],
                    w_send.at[number, step - 1], w_recv.at[number, step - 1], along_a(step)[1],
                )
            )
    for copy, _ in over_b:
        copy.wait()
    across = []
    for number, chunk in enumerate(CHUNKS):
        for copy in back[(SIDE - 1) * number : (SIDE - 1) * (number + 1)]:
            copy.wait_recv()
        across.append(
            send(
                wide.at[:, chunk], grads_ref.at[core, :, chunk],
                o_send.at[number], o_recv.at[number], sibling,
            )
        )
    stores.append(pltpu.make_async_copy(wide, grads_ref.at[core], store.at[1]))
    stores[1].start()
    for copy in back:
        copy.wait_send()
    for copy in across:
        copy.wait()
    for copy in stores:
        copy.wait()


def per_device(video, cotangent, weight_one, weight_two, predecessor, frame_count):
    frames, height, columns, width = video.shape[1:]
    groups, parts = lax.axis_size("tm"), lax.axis_size("space")
    scale = 1.0 / math.sqrt(groups * parts * frames * height * columns)
    far = pl.BlockSpec(memory_space=pltpu.HBM)
    dma = pltpu.SemaphoreType.DMA
    taps = weight_one.shape[0]
    blocks = (SIDE, BLOCK, WIDTH)
    output, grads = pl.pallas_call(
        lambda *refs: kernel(scale, *refs),
        out_shape=(
            jax.ShapeDtypeStruct(video.shape, HALF),
            jax.ShapeDtypeStruct((2,) + blocks, HALF),
        ),
        in_specs=[far] * 6,
        out_specs=(far, far),
        scratch_shapes=[
            pltpu.SMEM((1, 1), jnp.int32),
            pltpu.SMEM((1, 1), jnp.int32),
            pltpu.VMEM((FRAMES, LOW, COLS, WIDTH), HALF),
            pltpu.VMEM((taps, WIDTH), HALF),
            pltpu.VMEM((taps, WIDTH), HALF),
            pltpu.VMEM((FRAMES, LOW, COLS, WIDTH), HALF),
            pltpu.VMEM((FRAMES, LOW, COLS, WIDTH), HALF),
            pltpu.VMEM((2, FRAMES + 2, ROWS + 2, COLS, WIDTH), HALF),
            pltpu.VMEM((FRAMES + 4, ROWS + 2, COLS, WIDTH), HALF),
            pltpu.VMEM((2, ROWS, COLS, WIDTH), HALF),
            pltpu.VMEM((FRAMES, LOW, COLS, WIDTH), HALF),
            pltpu.VMEM((2, LOW, COLS, WIDTH), HALF),
            pltpu.VMEM((FRAMES * PLANE, WIDTH), FULL),
            pltpu.VMEM((2, FRAMES * PLANE, 3 * WIDTH), HALF),
            pltpu.VMEM((9 * WIDTH, WIDTH), FULL),
            pltpu.VMEM((SHARE, WIDTH), HALF),
            pltpu.VMEM((SHARE, WIDTH), HALF),
            pltpu.VMEM((SIDE * BLOCK, WIDTH), FULL),
            pltpu.VMEM(blocks, HALF),
            pltpu.VMEM((SIDE - 1, BLOCK, WIDTH), HALF),
            pltpu.VMEM(blocks, HALF),
            pltpu.VMEM(blocks, HALF),
            dma((6,)),
            dma((2,)),
            dma((SPACE - 1,)),
            dma((SPACE - 1,)),
            dma((SPACE,)),
            dma((SPACE,)),
            dma((SPACE - 1,)),
            dma((SPACE - 1,)),
            dma((SPACE,)),
            dma((SPACE,)),
            dma,
            dma,
            dma,
            dma,
            dma((len(CHUNKS),)),
            dma((len(CHUNKS),)),
            dma((len(CHUNKS),)),
            dma((len(CHUNKS),)),
            dma((len(CHUNKS), SIDE - 1)),
            dma((len(CHUNKS), SIDE - 1)),
            dma((2,)),
            dma((2,)),
        ],
        compiler_params=pltpu.CompilerParams(
            collective_id=0, has_side_effects=True, vmem_limit_bytes=62 * 1024 * 1024
        ),
    )(
        video, cotangent, weight_one, weight_two,
        predecessor.reshape(1, 1), frame_count.reshape(1, 1),
    )

    flat = grads.reshape(-1, WIDTH)

    def widened(number):
        begin = number * SIDE * BLOCK
        return flat[begin : begin + taps // parts].astype(FULL)

    return (output, widened(0), widened(1))


def solution(mesh):
    placed = (
        P("tm", None, "space", None, None),
        P("tm", None, "space", None, None),
        P(),
        P(),
        P("tm"),
        P("tm"),
    )
    return jax.shard_map(
        per_device,
        mesh=mesh,
        in_specs=placed,
        out_specs=(P("tm", None, "space", None, None), P("space", None), P("space", None)),
        check_vma=False,
    )
```
